128 devices in a mesh: section: 4 (over z), tensor: 8 (over y, x_lo), dp: 4 (over x_hi, core).
Axes of the slice: x: 4 (x_hi: 2, x_lo: 2; x = x_hi * 2 + x_lo), y: 4, z: 4, core: 2. Of those that a mesh axis runs over, the one named last changes fastest.
Arguments:
- queries: bfloat16 [4, 4, 3584, 8192], P('section', 'dp', None, 'tensor')
- grad_out: bfloat16 [4, 4, 3584, 8192], P('section', 'dp', None, 'tensor'), may hold values from -6 to 6
- tiles: bfloat16 [4, 512, 8192], P('dp', ('section', 'tensor')), may hold values from -6 to 6
- key_value_matrix: bfloat16 [4, 8192, 8, 2, 128], P('section', None, 'tensor'), may hold values from -0.0625 to 0.0625
- gate: float32 [4], P('section'), may hold values from 0.3 to 1.5
- tile_count: int32 [4], P('dp'), may hold values from 256 to 512, as said below
Outputs:
- query_grad: bfloat16 [4, 4, 3584, 8192], P('section', 'dp', None, 'tensor')
- tile_grad: bfloat16 [4, 512, 8192], P('dp', ('section', 'tensor'))
- weight_gradient: bfloat16 [4, 8192, 8, 2, 128], P('section', None, 'tensor')
The draws below stay inside these ranges and needn't reach their ends.
Inputs may be any that keep to these rules, and one draw needn't show every extreme that they name: `tile_count`: each report has 256 to 512 valid tiles, and one report has all 512.
All inputs are finite; a program needn't handle non-finite values.
Results may differ from the reference program's by a relative error of at most 0.039.
The reference program's roundings to bfloat16 on the way count: a program that leaves them out, or rounds other values in their place, can miss the bound.
Values may be sent and summed in bfloat16 or wider, within the bound.
A program may use at most 192 MiB of HBM per device.

```python
import jax
import jax.numpy as jnp
from jax import lax

MODEL_DIMENSION = 8192
HQ = 64
KEY_VALUE_HEADS = 8
HEAD_SIZE = 128
TEXT_TOKENS = 3584
TILE_TOKENS = 512
QUERY_GROUP = 8
CROSS_LAYERS = 4
REPORTS = 4


def draw_queries(key, part):
    key = jax.random.fold_in(key, 11)
    key_base, key_scale = jax.random.split(key, 2)
    array_shape = (CROSS_LAYERS, REPORTS, TEXT_TOKENS, HQ * HEAD_SIZE)
    row_shape = (CROSS_LAYERS, REPORTS, TEXT_TOKENS, 1)
    base_values = jnp.clip(jax.random.normal(key_base, array_shape, jnp.float32), -6.0, 6.0)
    row_scale = jnp.exp(jax.random.uniform(key_scale, row_shape, jnp.float32, -0.69, 1.1))
    return (base_values * row_scale).astype(jnp.bfloat16)


def draw_tile_count(key, part):
    key = jax.random.fold_in(key, 7)
    key_lengths, key_full = jax.random.split(key)
    counts = jax.random.randint(key_lengths, (REPORTS,), TILE_TOKENS // 2, TILE_TOKENS + 1)
    full_report = jax.random.randint(key_full, (), 0, REPORTS)
    return jnp.where(jnp.arange(REPORTS) == full_report, TILE_TOKENS, counts).astype(jnp.int32)


def levels(own_key, shape, pieces, least, high):
    level, own = 1.0, jax.random.fold_in(own_key, 6)
    for axis_at, shards_of in pieces:
        steps = jnp.exp(jax.random.uniform(jax.random.fold_in(own, axis_at), (shards_of,), jnp.float32, least / len(pieces), high / len(pieces)))
        level = level * jnp.repeat(steps, shape[axis_at] // shards_of).reshape([-1 if axis == axis_at else 1 for axis in range(len(shape))])
    return level


def normal_values(rng, shape, scale, limit, cuts=(), kind=jnp.bfloat16):
    loudness = levels(rng, shape, cuts, -0.22, 0.18) if cuts else 1.0
    result = jax.random.normal(rng, shape, jnp.float32) * scale * loudness
    return jnp.minimum(jnp.maximum(result, -limit), limit).astype(kind)


def setup_inputs(seed: int = 0) -> dict:
    key_list = jax.random.split(jax.random.key(seed), 7)
    return {
        "queries": draw_queries(jax.random.fold_in(key_list[6], 71), 0),
        "grad_out": normal_values(key_list[1], (CROSS_LAYERS, REPORTS, TEXT_TOKENS, HQ * HEAD_SIZE), 1.0, 6.0, ((0, 4), (1, 4), (3, 8))),
        "tiles": normal_values(key_list[2], (REPORTS, TILE_TOKENS, MODEL_DIMENSION), 1.0, 6.0, ((0, 4), (1, 32))),
        "key_value_matrix": normal_values(key_list[3], (CROSS_LAYERS, MODEL_DIMENSION, KEY_VALUE_HEADS, 2, HEAD_SIZE), MODEL_DIMENSION ** -0.5, 0.0625, ((0, 4), (2, 8))),
        "gate": jnp.clip(0.3 + 1.2 * jax.random.uniform(key_list[4], (CROSS_LAYERS,), jnp.float32) ** levels(key_list[4], (CROSS_LAYERS,), ((0, 4),), -0.2, 0.2), 0.3, 1.5),
        "tile_count": draw_tile_count(jax.random.fold_in(key_list[6], 71), 0),
    }


def group_grads(query_block, grad_block, key_rows, value_rows, tile_valid, score_scale):
    query_wide = query_block.astype(jnp.float32)
    grad_wide = grad_block.astype(jnp.float32)
    key_wide = key_rows.astype(jnp.float32)
    value_wide = value_rows.astype(jnp.float32)
    scores = jnp.einsum("igd,jd->gij", query_wide, key_wide) * score_scale
    scores = jnp.where(tile_valid[None, None, :], scores, -jnp.inf)
    row_max = jnp.max(scores, axis=2, keepdims=True)
    exp_scores = jnp.exp(scores - row_max)
    softmax_rows = exp_scores / jnp.sum(exp_scores, axis=2, keepdims=True)
    probs_half = softmax_rows.astype(jnp.bfloat16)
    dprobs = jnp.einsum("igd,jd->gij", grad_wide, value_wide)
    row_delta = jnp.sum(softmax_rows * dprobs, axis=2, keepdims=True)
    dscores = (softmax_rows * (dprobs - row_delta) * score_scale).astype(jnp.bfloat16)
    dscores_wide = dscores.astype(jnp.float32)
    query_part = jnp.einsum("gij,jd->igd", dscores_wide, key_wide).astype(jnp.bfloat16)
    key_grad = jnp.einsum("gij,igd->jd", dscores_wide, query_wide)
    value_grad = jnp.einsum("gij,igd->jd", probs_half.astype(jnp.float32), grad_wide)
    return query_part, jnp.concatenate([key_grad, value_grad], axis=1)


def reference(queries, grad_out, tiles, key_value_matrix, gate, tile_count):
    score_scale = HEAD_SIZE ** -0.5
    paired_width = KEY_VALUE_HEADS * 2 * HEAD_SIZE
    query_lists = [[None] * REPORTS for section_layer_index in range(CROSS_LAYERS)]
    weight_running_sums = [jnp.zeros((MODEL_DIMENSION, paired_width), jnp.float32) for section_layer_index in range(CROSS_LAYERS)]
    tile_parts = []
    for report_index in range(REPORTS):
        tile_valid = jnp.arange(TILE_TOKENS, dtype=jnp.int32) < tile_count[report_index]
        tile_sum = jnp.zeros((TILE_TOKENS, MODEL_DIMENSION), jnp.float32)
        for section_layer_index in range(CROSS_LAYERS):
            weight = key_value_matrix[section_layer_index].reshape(MODEL_DIMENSION, paired_width)
            projected_key_values = jnp.dot(tiles[report_index], weight, preferred_element_type=jnp.float32).astype(jnp.bfloat16)
            paired_heads = projected_key_values.reshape(TILE_TOKENS, KEY_VALUE_HEADS, 2, HEAD_SIZE).transpose(1, 0, 2, 3)
            query_row_block = queries[section_layer_index, report_index].reshape(TEXT_TOKENS, KEY_VALUE_HEADS, QUERY_GROUP, HEAD_SIZE).transpose(1, 0, 2, 3)
            factor = jnp.tanh(gate[section_layer_index])
            gradient_heads = (factor * grad_out[section_layer_index, report_index].astype(jnp.float32)).astype(jnp.bfloat16)
            gradient_rows = gradient_heads.reshape(TEXT_TOKENS, KEY_VALUE_HEADS, QUERY_GROUP, HEAD_SIZE).transpose(1, 0, 2, 3)

            def one_group(inputs):
                query_block, grad_block, pair_block = inputs
                return group_grads(query_block, grad_block, pair_block[:, 0], pair_block[:, 1], tile_valid, score_scale)

            query_part, pair_part = lax.map(one_group, (query_row_block, gradient_rows, paired_heads))
            query_lists[section_layer_index][report_index] = query_part.transpose(1, 0, 2, 3).reshape(TEXT_TOKENS, HQ * HEAD_SIZE)
            pair_grad = pair_part.astype(jnp.bfloat16).transpose(1, 0, 2).reshape(TILE_TOKENS, paired_width)
            tile_sum = tile_sum + lax.dot_general(pair_grad, weight, (((1,), (1,)), ((), ())), preferred_element_type=jnp.float32)
            weight_running_sums[section_layer_index] = weight_running_sums[section_layer_index] + lax.dot_general(tiles[report_index], pair_grad, (((0,), (0,)), ((), ())), preferred_element_type=jnp.float32)
        tile_parts.append(tile_sum.astype(jnp.bfloat16))
    query_grad = jnp.stack([jnp.stack(query_lists[section_layer_index], axis=0) for section_layer_index in range(CROSS_LAYERS)], axis=0)
    tile_grad = jnp.stack(tile_parts, axis=0)
    weight_gradient = jnp.stack([weight_running_sums[section_layer_index].astype(jnp.bfloat16).reshape(MODEL_DIMENSION, KEY_VALUE_HEADS, 2, HEAD_SIZE) for section_layer_index in range(CROSS_LAYERS)], axis=0)
    return query_grad, tile_grad, weight_gradient
```

```python
import functools
import heapq

import jax
import jax.numpy as jnp
from jax import lax
from jax.experimental import pallas as pl
from jax.experimental.pallas import tpu as pltpu
from jax.sharding import PartitionSpec as P

F32, BF = jnp.float32, jnp.bfloat16
SC = 128 ** -0.5
LOG2E = 1.4426950408889634


def dg(a, b, ca, cb):
    return lax.dot_general(a, b, (((ca,), (cb,)), ((), ())), preferred_element_type=F32)

MESH = pl.DeviceIdType.MESH
SIZES = {"z": 4, "y": 4, "x": 2}
AX = "zyx"

def gather_plan(parts, latency=0.3):
    def dirs(a):
        return (1,) if SIZES[a] == 2 else (1, -1)
    def shift(u, a, s):
        u = list(u); n = AX.index(a); u[n] = (u[n] - s) % SIZES[a]
        return tuple(u)
    def sends_of(p, u, via):
        order, _, flip = parts[p]
        out = []
        if via is not None:
            a, s = via
            k = order.index(a)
            if SIZES[a] == 4 and u[AX.index(a)] in (1, 3):
                d = -1 if u[AX.index(a)] == 1 else 1
                par = (sum(u[AX.index(b)] for b in order[:k]) + flip) % 2
                if (d == 1) == (par == 0):
                    out.append((p, u, a, d))
            rest = order[k + 1:]
        else:
            rest = order
        for a in rest:
            for d in dirs(a):
                out.append((p, u, a, d))
        return out
    free = {}
    heap = []
    cnt = 0
    def push(t, sends):
        nonlocal cnt
        for (p, u, a, d) in sends:
            t0 = max(t, free.get((a, d), 0.0))
            t1 = t0 + parts[p][1]
            free[(a, d)] = t1
            cnt += 1
            heapq.heappush(heap, (t1 + latency, cnt, p, shift(u, a, d), (a, d)))
    init = [s for p in range(len(parts)) for s in sends_of(p, (0, 0, 0), None)]
    push(0.0, init)
    events, last = [], 0.0
    while heap:
        t, _, p, u, via = heapq.heappop(heap)
        s = sends_of(p, u, via)
        events.append((t, p, u, s))
        push(t, s)
        last = t
    for p in range(len(parts)):
        got = sorted(u for _, q, u, _ in events if q == p)
        assert len(got) == 31 and len(set(got)) == 31, (p, len(got), len(set(got)))
    return init, events, last, dict(free)

def place():
    z = lax.axis_index("section"); t = lax.axis_index("tensor")
    return z, t // 2, t % 2

def neighbour(zyx, a, d):
    z, y, x = zyx
    if a == "z":
        return {"section": (z + d) % 4}
    if a == "y":
        return {"tensor": ((y + d) % 4) * 2 + x}
    return {"tensor": y * 2 + (1 - x)}

def uidx(u):
    return u[0] * 8 + u[1] * 2 + u[2]

def row_of(zyx, u):
    z, y, x = zyx
    return ((z + u[0]) % 4) * 8 + ((y + u[1]) % 4) * 2 + (x + u[2]) % 2

def greet(zyx):
    bar = pltpu.get_barrier_semaphore()
    ns = [("x", 1), ("y", 1), ("y", -1), ("z", 1), ("z", -1)]
    for a, d in ns:
        pl.semaphore_signal(bar, inc=1, device_id=neighbour(zyx, a, d), device_id_type=MESH)
    pl.semaphore_wait(bar, len(ns))

PARTS = {4: [("xyz", 0.6875, 0), ("xzy", 0.6875, 0), ("yzx", 0.3125, 0), ("zyx", 0.3125, 1)]}
COLS = {4: [(0, 2816), (2816, 2816), (5632, 1280), (6912, 1280)]}

def ag_kernel(np_, tiles_ref, out_ref, send_sem, recv_sem, loc_sem):
    zyx = place()
    init, events, _, _ = gather_plan(PARTS[np_])
    cols = COLS[np_]
    greet(zyx)
    mine = row_of(zyx, (0, 0, 0))
    loc = pltpu.make_async_copy(tiles_ref.at[0], out_ref.at[pl.ds(pl.multiple_of(mine * 16, 16), 16)], loc_sem)
    loc.start()
    started = []
    def view(ref, p, u):
        return ref.at[pl.ds(pl.multiple_of(row_of(zyx, u) * 16, 16), 16), pl.ds(*cols[p])]
    def start(p, u, a, d):
        n = AX.index(a); v = list(u); v[n] = (v[n] - d) % SIZES[a]
        src = tiles_ref.at[0, :, pl.ds(*cols[p])] if u == (0, 0, 0) else view(out_ref, p, u)
        c = pltpu.make_async_remote_copy(src_ref=src, dst_ref=view(out_ref, p, u),
            send_sem=send_sem.at[len(started)], recv_sem=recv_sem.at[p * 32 + uidx(v)],
            device_id=neighbour(zyx, a, d), device_id_type=MESH)
        c.start(); started.append(c)
    def wait(p, u):
        v = view(out_ref, p, u)
        pltpu.make_async_copy(v, v, recv_sem.at[p * 32 + uidx(u)]).wait()
    for s in init: start(*s)
    for _, p, u, sends in events:
        wait(p, u)
        for s in sends: start(*s)
    for c in started: c.wait_send()
    loc.wait()

def nsends(np_):
    init, events, _, _ = gather_plan(PARTS[np_])
    return len(init) + sum(len(e[3]) for e in events)

def all_gather_tiles(tiles, np_=4, cid=0):
    return pl.pallas_call(
        functools.partial(ag_kernel, np_),
        in_specs=[pl.BlockSpec(memory_space=pl.ANY)],
        out_specs=pl.BlockSpec(memory_space=pl.ANY),
        out_shape=jax.ShapeDtypeStruct((512, 8192), jnp.bfloat16),
        scratch_shapes=[pltpu.SemaphoreType.DMA((nsends(np_),)), pltpu.SemaphoreType.DMA((np_ * 32,)), pltpu.SemaphoreType.DMA],
        compiler_params=pltpu.CompilerParams(collective_id=cid, has_side_effects=True),
    )(tiles)

def attention_rows(lay, sub, f, cnt, q_ref, g_ref, kv_ref, dq_ref, ka, va, opt=""):
    k = kv_ref[:, :128]; v = kv_ref[:, 128:]
    J = k.shape[0]; R = q_ref.shape[0]; H = J // 2
    ax = 0 if lay == "T" else 1
    valid = lax.broadcasted_iota(jnp.int32, (H, 1) if ax == 0 else (1, H), ax) + H < cnt
    items = [(h, r) for r in range(R // sub) for h in range(8)]
    def first(it):
        h, r = it
        rs = pl.ds(r * sub, sub); c = pl.ds(h * 128, 128)
        q = q_ref[rs, c]; g = (f * g_ref[rs, c].astype(F32)).astype(BF)
        if lay == "T": return q, g, dg(k, q, 1, 1), dg(v, g, 1, 1)
        return q, g, dg(q, k, 1, 1), dg(g, v, 1, 1)
    def mid(q, g, s, dp):
        if ax == 0: s = jnp.concatenate([s[:H], jnp.where(valid, s[H:], -jnp.inf)], axis=0)
        else: s = jnp.concatenate([s[:, :H], jnp.where(valid, s[:, H:], -jnp.inf)], axis=1)
        m = jnp.max(s, axis=ax, keepdims=True)
        e = jnp.exp2((s - m) * (SC * LOG2E))
        inv = 1.0 / jnp.sum(e, axis=ax, keepdims=True)
        delta = jnp.sum(e * dp, axis=ax, keepdims=True) * inv
        ph = (e * inv).astype(BF)
        ds = ((e * (inv * SC)) * (dp - delta)).astype(BF)
        return ds, ph
    def last(it, q, g, ds, ph):
        h, r = it
        o = (pl.ds(r * sub, sub), pl.ds(h * 128, 128))
        if lay == "T":
            dq_ref[o] = dg(k, ds, 0, 0).T.astype(BF)
            ka[...] += dg(ds, q, 1, 0); va[...] += dg(ph, g, 1, 0)
        else:
            dq_ref[o] = dg(ds, k, 1, 0).astype(BF)
            ka[...] += dg(q, ds, 0, 0); va[...] += dg(g, ph, 0, 0)
    nxt = first(items[0]); prev = None
    for n, it in enumerate(items):
        cur = nxt
        if n + 1 < len(items): nxt = first(items[n + 1])
        if prev is not None: last(*prev)
        b = mid(*cur)
        prev = (it, cur[0], cur[1], *b)
    last(*prev)
def attention_kernel(lay, sub, cnt_ref, fac_ref, q_ref, g_ref, kv_ref, dq_ref, pair_ref, ka, va):
    i = pl.program_id(0)
    @pl.when(i == 0)
    def _():
        ka[...] = jnp.zeros_like(ka); va[...] = jnp.zeros_like(va)
    attention_rows(lay, sub, fac_ref[0], cnt_ref[0], q_ref, g_ref, kv_ref, dq_ref, ka, va)
    @pl.when(i == pl.num_programs(0) - 1)
    def _():
        a, b = ka[...], va[...]
        if lay == "L": a, b = a.T, b.T
        pair_ref[:, :128] = a.astype(BF); pair_ref[:, 128:] = b.astype(BF)
def attention(q, g, kv, cnt, fac, lay="T", R=512, sub=512):
    n = q.shape[0]
    return pl.pallas_call(
        functools.partial(attention_kernel, lay, sub),
        grid=(n // R,),
        in_specs=[pl.BlockSpec(memory_space=pltpu.SMEM)] * 2 + [
            pl.BlockSpec((R, 1024), lambda i: (i, 0)),
            pl.BlockSpec((R, 1024), lambda i: (i, 0)),
            pl.BlockSpec((512, 256), lambda i: (0, 0))],
        out_specs=[pl.BlockSpec((R, 1024), lambda i: (i, 0)), pl.BlockSpec((512, 256), lambda i: (0, 0))],
        out_shape=[jax.ShapeDtypeStruct((n, 1024), BF), jax.ShapeDtypeStruct((512, 256), BF)],
        scratch_shapes=[pltpu.VMEM((512, 128) if lay == "T" else (128, 512), F32)] * 2,
        compiler_params=pltpu.CompilerParams(vmem_limit_bytes=60 * 2**20, dimension_semantics=("arbitrary",)),
    )(cnt, fac, q, g, kv)


def local(queries, grad_out, tiles, key_value_matrix, gate, tile_count):
    weight = key_value_matrix[0].reshape(8192, 256)
    every_tile = all_gather_tiles(tiles)
    kv = jnp.dot(every_tile, weight, preferred_element_type=F32).astype(BF)
    query_grad, pair = attention(
        queries[0, 0], grad_out[0, 0], kv, tile_count, jnp.tanh(gate), lay="L", R=512, sub=512
    )
    tile_sum = lax.psum_scatter(
        dg(pair, weight, 1, 1).astype(BF), ("section", "tensor"), scatter_dimension=0, tiled=True
    )
    weight_total = lax.psum(dg(every_tile, pair, 0, 0).astype(BF), "dp")
    return (query_grad[None, None], tile_sum[None], weight_total.reshape(1, 8192, 1, 2, 128))


def solution(mesh):
    return jax.shard_map(
        local,
        mesh=mesh,
        in_specs=(
            P("section", "dp", None, "tensor"),
            P("section", "dp", None, "tensor"),
            P("dp", ("section", "tensor"), None),
            P("section", None, "tensor", None, None),
            P("section"),
            P("dp"),
        ),
        out_specs=(
            P("section", "dp", None, "tensor"),
            P("dp", ("section", "tensor"), None),
            P("section", None, "tensor", None, None),
        ),
        check_vma=False,
    )
```

```python
import functools
import heapq

import jax
import jax.numpy as jnp
from jax import lax
from jax.experimental import pallas as pl
from jax.experimental.pallas import tpu as pltpu
from jax.sharding import PartitionSpec as P

F32, BF = jnp.float32, jnp.bfloat16
SC = 128 ** -0.5
LOG2E = 1.4426950408889634


def dg(a, b, ca, cb):
    return lax.dot_general(a, b, (((ca,), (cb,)), ((), ())), preferred_element_type=F32)

MESH = pl.DeviceIdType.MESH
SIZES = {"z": 4, "y": 4, "x": 2}
AX = "zyx"

def gather_plan(parts, latency=0.3):
    def dirs(a):
        return (1,) if SIZES[a] == 2 else (1, -1)
    def shift(u, a, s):
        u = list(u); n = AX.index(a); u[n] = (u[n] - s) % SIZES[a]
        return tuple(u)
    def sends_of(p, u, via):
        order, _, flip = parts[p]
        out = []
        if via is not None:
            a, s = via
            k = order.index(a)
            if SIZES[a] == 4 and u[AX.index(a)] in (1, 3):
                d = -1 if u[AX.index(a)] == 1 else 1
                par = (sum(u[AX.index(b)] for b in order[:k]) + flip) % 2
                if (d == 1) == (par == 0):
                    out.append((p, u, a, d))
            rest = order[k + 1:]
        else:
            rest = order
        for a in rest:
            for d in dirs(a):
                out.append((p, u, a, d))
        return out
    free = {}
    heap = []
    cnt = 0
    def push(t, sends):
        nonlocal cnt
        for (p, u, a, d) in sends:
            t0 = max(t, free.get((a, d), 0.0))
            t1 = t0 + parts[p][1]
            free[(a, d)] = t1
            cnt += 1
            heapq.heappush(heap, (t1 + latency, cnt, p, shift(u, a, d), (a, d)))
    init = [s for p in range(len(parts)) for s in sends_of(p, (0, 0, 0), None)]
    push(0.0, init)
    events, last = [], 0.0
    while heap:
        t, _, p, u, via = heapq.heappop(heap)
        s = sends_of(p, u, via)
        events.append((t, p, u, s))
        push(t, s)
        last = t
    for p in range(len(parts)):
        got = sorted(u for _, q, u, _ in events if q == p)
        assert len(got) == 31 and len(set(got)) == 31, (p, len(got), len(set(got)))
    return init, events, last, dict(free)

def place():
    z = lax.axis_index("section"); t = lax.axis_index("tensor")
    return z, t // 2, t % 2

def neighbour(zyx, a, d):
    z, y, x = zyx
    if a == "z":
        return {"section": (z + d) % 4}
    if a == "y":
        return {"tensor": ((y + d) % 4) * 2 + x}
    return {"tensor": y * 2 + (1 - x)}

def uidx(u):
    return u[0] * 8 + u[1] * 2 + u[2]

def row_of(zyx, u):
    z, y, x = zyx
    return ((z + u[0]) % 4) * 8 + ((y + u[1]) % 4) * 2 + (x + u[2]) % 2

def greet(zyx):
    bar = pltpu.get_barrier_semaphore()
    ns = [("x", 1), ("y", 1), ("y", -1), ("z", 1), ("z", -1)]
    for a, d in ns:
        pl.semaphore_signal(bar, inc=1, device_id=neighbour(zyx, a, d), device_id_type=MESH)
    pl.semaphore_wait(bar, len(ns))

PARTS = {4: [("xyz", 0.6875, 0), ("xzy", 0.6875, 0), ("yzx", 0.3125, 0), ("zyx", 0.3125, 1)]}
COLS = {4: [(0, 2816), (2816, 2816), (5632, 1280), (6912, 1280)]}

def ag_kernel(np_, tiles_ref, out_ref, send_sem, recv_sem, loc_sem):
    zyx = place()
    init, events, _, _ = gather_plan(PARTS[np_])
    cols = COLS[np_]
    greet(zyx)
    mine = row_of(zyx, (0, 0, 0))
    loc = pltpu.make_async_copy(tiles_ref.at[0], out_ref.at[pl.ds(pl.multiple_of(mine * 16, 16), 16)], loc_sem)
    loc.start()
    started = []
    def view(ref, p, u):
        return ref.at[pl.ds(pl.multiple_of(row_of(zyx, u) * 16, 16), 16), pl.ds(*cols[p])]
    def start(p, u, a, d):
        n = AX.index(a); v = list(u); v[n] = (v[n] - d) % SIZES[a]
        src = tiles_ref.at[0, :, pl.ds(*cols[p])] if u == (0, 0, 0) else view(out_ref, p, u)
        c = pltpu.make_async_remote_copy(src_ref=src, dst_ref=view(out_ref, p, u),
            send_sem=send_sem.at[len(started)], recv_sem=recv_sem.at[p * 32 + uidx(v)],
            device_id=neighbour(zyx, a, d), device_id_type=MESH)
        c.start(); started.append(c)
    def wait(p, u):
        v = view(out_ref, p, u)
        pltpu.make_async_copy(v, v, recv_sem.at[p * 32 + uidx(u)]).wait()
    for s in init: start(*s)
    for _, p, u, sends in events:
        wait(p, u)
        for s in sends: start(*s)
    for c in started: c.wait_send()
    loc.wait()

def nsends(np_):
    init, events, _, _ = gather_plan(PARTS[np_])
    return len(init) + sum(len(e[3]) for e in events)

def all_gather_tiles(tiles, np_=4, cid=0):
    return pl.pallas_call(
        functools.partial(ag_kernel, np_),
        in_specs=[pl.BlockSpec(memory_space=pl.ANY)],
        out_specs=pl.BlockSpec(memory_space=pl.ANY),
        out_shape=jax.ShapeDtypeStruct((512, 8192), jnp.bfloat16),
        scratch_shapes=[pltpu.SemaphoreType.DMA((nsends(np_),)), pltpu.SemaphoreType.DMA((np_ * 32,)), pltpu.SemaphoreType.DMA],
        compiler_params=pltpu.CompilerParams(collective_id=cid, has_side_effects=True),
    )(tiles)

def attention_rows(lay, sub, f, cnt, q_ref, g_ref, kv_ref, dq_ref, ka, va, opt=""):
    k = kv_ref[:, :128]; v = kv_ref[:, 128:]
    J = k.shape[0]; R = q_ref.shape[0]; H = J // 2
    ax = 0 if lay == "T" else 1
    valid = lax.broadcasted_iota(jnp.int32, (H, 1) if ax == 0 else (1, H), ax) + H < cnt
    items = [(h, r) for r in range(R // sub) for h in range(8)]
    def first(it):
        h, r = it
        rs = pl.ds(r * sub, sub); c = pl.ds(h * 128, 128)
        q = q_ref[rs, c]; g = (f * g_ref[rs, c].astype(F32)).astype(BF)
        if lay == "T": return q, g, dg(k, q, 1, 1), dg(v, g, 1, 1)
        return q, g, dg(q, k, 1, 1), dg(g, v, 1, 1)
    def mid(q, g, s, dp):
        if ax == 0: s = jnp.concatenate([s[:H], jnp.where(valid, s[H:], -jnp.inf)], axis=0)
        else: s = jnp.concatenate([s[:, :H], jnp.where(valid, s[:, H:], -jnp.inf)], axis=1)
        m = jnp.max(s, axis=ax, keepdims=True)
        e = jnp.exp2((s - m) * (SC * LOG2E))
        inv = 1.0 / jnp.sum(e, axis=ax, keepdims=True)
        delta = jnp.sum(e * dp, axis=ax, keepdims=True) * inv
        ph = (e * inv).astype(BF)
        ds = ((e * (inv * SC)) * (dp - delta)).astype(BF)
        return ds, ph
    def last(it, q, g, ds, ph):
        h, r = it
        o = (pl.ds(r * sub, sub), pl.ds(h * 128, 128))
        if lay == "T":
            dq_ref[o] = dg(k, ds, 0, 0).T.astype(BF)
            ka[...] += dg(ds, q, 1, 0); va[...] += dg(ph, g, 1, 0)
        else:
            dq_ref[o] = dg(ds, k, 1, 0).astype(BF)
            ka[...] += dg(q, ds, 0, 0); va[...] += dg(g, ph, 0, 0)
    nxt = first(items[0]); prev = None
    for n, it in enumerate(items):
        cur = nxt
        if n + 1 < len(items): nxt = first(items[n + 1])
        if prev is not None: last(*prev)
        b = mid(*cur)
        prev = (it, cur[0], cur[1], *b)
    last(*prev)


def background_plan(steps, unit_us=1.46, start_us=6.0, step_us=3.4):
    parts = [("xzy", 1.0, 0), ("xzy", 1.0, 1)]
    init, events, _, _ = gather_plan(parts, latency=1.5)
    per_step = [[] for _ in range(steps)]
    for t, p, u, sends in events:
        n = int((start_us + t * unit_us) / step_us) + 1
        per_step[min(n, steps - 1)].append((p, u, sends))
    return init, per_step


def count_sends(init, per_step):
    return len(init) + sum(len(e[2]) for b in per_step for e in b)


def greet_all(zyx):
    z, y, x = zyx
    dp = lax.axis_index("dp")
    peers = [{"section": (z + d) % 4} for d in (1, 2, 3)]
    peers += [{"tensor": ((y + d) % 4) * 2 + x} for d in (1, 2, 3)]
    peers += [{"tensor": y * 2 + (1 - x)}]
    peers += [{"dp": dp ^ k} for k in (1, 2, 3)]
    bar = pltpu.get_barrier_semaphore()
    for d in peers:
        pl.semaphore_signal(bar, inc=1, device_id=d, device_id_type=MESH)
    pl.semaphore_wait(bar, len(peers))


def attention_kernel(steps, cnt_ref, fac_ref, q_ref, g_ref, kv_ref, tiles_ref, all_ref, w_ref,
                     dq_ref, pair_ref, others_ref, wz_ref, ka, va,
                     send_sem, recv_sem, swap_send, swap_recv, w_send, w_recv, c_send, c_recv, x_send, x_recv):
    i = pl.program_id(0)
    zyx = place()
    z = zyx[0]
    dp = lax.axis_index("dp")
    core = dp % 2
    init, per_step = background_plan(steps)
    started = []

    def rows(u):
        return pl.ds(pl.multiple_of(row_of(zyx, u) * 16, 16), 16)

    def quarter(d):
        return pl.ds(pl.multiple_of(d * 2048, 2048), 2048)

    def part_copy(p, u, a, d, at=None):
        if at is None:
            at = len(started)
            started.append((p, u, a, d, at))
        n = AX.index(a)
        v = list(u)
        v[n] = (v[n] - d) % SIZES[a]
        c = pltpu.make_async_remote_copy(
            src_ref=others_ref.at[p, rows(u)], dst_ref=others_ref.at[p, rows(u)],
            send_sem=send_sem.at[at], recv_sem=recv_sem.at[p * 32 + uidx(v)],
            device_id=neighbour(zyx, a, d), device_id_type=MESH)
        return c

    def landed(ref, sem):
        pltpu.make_async_copy(ref, ref, sem).wait()

    def swap(p):
        return pltpu.make_async_remote_copy(
            src_ref=tiles_ref.at[0, :, quarter(dp ^ (2 + p))], dst_ref=others_ref.at[p, rows((0, 0, 0))],
            send_sem=swap_send.at[p], recv_sem=swap_recv.at[p], device_id={"dp": dp ^ (2 + p)}, device_id_type=MESH)

    def w_copy(d):
        t = (z + d) % 4
        return pltpu.make_async_remote_copy(
            src_ref=w_ref.at[pl.ds(pl.multiple_of(t * 2048 + core * 1024, 1024), 1024)],
            dst_ref=wz_ref.at[4 - d, pl.ds(pl.multiple_of(core * 1024, 1024), 1024)],
            send_sem=w_send.at[d - 1], recv_sem=w_recv.at[3 - d], device_id={"section": t}, device_id_type=MESH)

    def c_copy(k):
        half = wz_ref.at[k, pl.ds(pl.multiple_of(core * 1024, 1024), 1024)]
        return pltpu.make_async_remote_copy(
            src_ref=half, dst_ref=half, send_sem=c_send.at[k - 1], recv_sem=c_recv.at[k - 1],
            device_id={"dp": dp ^ 1}, device_id_type=MESH)

    def x_copy():
        return pltpu.make_async_remote_copy(
            src_ref=all_ref.at[:, quarter(dp ^ 1)], dst_ref=others_ref.at[2],
            send_sem=x_send, recv_sem=x_recv, device_id={"dp": dp ^ 1}, device_id_type=MESH)

    @pl.when(i == 0)
    def _():
        ka[...] = jnp.zeros_like(ka)
        va[...] = jnp.zeros_like(va)
        greet_all(zyx)
        for p in (0, 1):
            swap(p).start()
        for d in (1, 3, 2):
            w_copy(d).start()
        x_copy().start()

    for n in range(1, steps):
        def batch(n=n):
            if n == 2:
                for p in (0, 1):
                    landed(others_ref.at[p, rows((0, 0, 0))], swap_recv.at[p])
                for s in init:
                    part_copy(*s).start()
            for p, u, sends in per_step[n]:
                landed(others_ref.at[p, rows(u)], recv_sem.at[p * 32 + uidx(u)])
                for s in sends:
                    part_copy(*s).start()
            if n == steps - 2:
                for k in (1, 3, 2):
                    half = wz_ref.at[k, pl.ds(pl.multiple_of(core * 1024, 1024), 1024)]
                    landed(half, w_recv.at[k - 1])
                    c_copy(k).start()
        if n == 2 or per_step[n] or n == steps - 2:
            assert n >= 2
            pl.when(i == n)(batch)

    attention_rows("L", q_ref.shape[0], fac_ref[0], cnt_ref[0], q_ref, g_ref, kv_ref, dq_ref, ka, va)

    @pl.when(i == steps - 1)
    def _():
        pair_ref[:, :128] = ka[...].T.astype(BF)
        pair_ref[:, 128:] = va[...].T.astype(BF)
        for s in started:
            part_copy(*s).wait_send()
        for p in (0, 1):
            swap(p).wait_send()
        for d in (1, 2, 3):
            w_copy(d).wait_send()
        for k in (1, 2, 3):
            c_copy(k).wait_send()
            half = wz_ref.at[k, pl.ds(pl.multiple_of((1 - core) * 1024, 1024), 1024)]
            landed(half, c_recv.at[k - 1])
        x_copy().wait()


def attention(q, g, kv, cnt, fac, tiles, every_tile, weight, R=256):
    n = q.shape[0]
    steps = n // R
    hbm = pl.BlockSpec(memory_space=pl.ANY)
    dma = pltpu.SemaphoreType.DMA
    return pl.pallas_call(
        functools.partial(attention_kernel, steps),
        grid=(steps,),
        in_specs=[pl.BlockSpec(memory_space=pltpu.SMEM)] * 2 + [
            pl.BlockSpec((R, 1024), lambda i: (i, 0)),
            pl.BlockSpec((R, 1024), lambda i: (i, 0)),
            pl.BlockSpec((512, 256), lambda i: (0, 0)), hbm, hbm, hbm],
        out_specs=[pl.BlockSpec((R, 1024), lambda i: (i, 0)), pl.BlockSpec((512, 256), lambda i: (0, 0)), hbm, hbm],
        out_shape=[jax.ShapeDtypeStruct((n, 1024), BF), jax.ShapeDtypeStruct((512, 256), BF),
                   jax.ShapeDtypeStruct((3, 512, 2048), BF), jax.ShapeDtypeStruct((4, 2048, 2, 128), BF)],
        scratch_shapes=[pltpu.VMEM((128, 512), F32)] * 2 + [
            dma((count_sends(*background_plan(steps)),)), dma((64,)), dma((2,)), dma((2,)), dma((3,)), dma((3,)),
            dma((3,)), dma((3,)), dma, dma],
        compiler_params=pltpu.CompilerParams(
            vmem_limit_bytes=60 * 2**20, dimension_semantics=("arbitrary",), collective_id=1, has_side_effects=True),
    )(cnt, fac, q, g, kv, tiles, every_tile, weight)


def tail_kernel(pair_ref, others_ref, all_ref, wz_ref, w_ref, tg_ref, wg_ref,
                pz, pr, gq, wv, wq, tp, rs, own, xs, xr, zs,
                l_sem, p_send, p_recv, f_send, f_recv, g_send, g_recv, h_send, h_recv,
                y_send, y_recv, x_send, x_recv, z_send, z_recv, o_sem):
    zyx = place()
    z, y, x = zyx
    dp = lax.axis_index("dp")

    def remote(src, dst, ss, rs_, dev):
        return pltpu.make_async_remote_copy(
            src_ref=src, dst_ref=dst, send_sem=ss, recv_sem=rs_, device_id=dev, device_id_type=MESH)

    loads = [pltpu.make_async_copy(pair_ref, pr.at[0], l_sem.at[0]),
             pltpu.make_async_copy(pair_ref, pz.at[0], l_sem.at[1]),
             pltpu.make_async_copy(all_ref.at[:, pl.ds(pl.multiple_of(dp * 2048, 2048), 2048)], gq.at[0], l_sem.at[2]),
             pltpu.make_async_copy(others_ref.at[2], gq.at[1], l_sem.at[3]),
             pltpu.make_async_copy(others_ref.at[0], gq.at[2], l_sem.at[4]),
             pltpu.make_async_copy(others_ref.at[1], gq.at[3], l_sem.at[5]),
             pltpu.make_async_copy(w_ref.at[pl.ds(pl.multiple_of(z * 2048, 2048), 2048)], wv.at[0], l_sem.at[6])]
    loads += [pltpu.make_async_copy(wz_ref.at[k], wv.at[k], l_sem.at[6 + k]) for k in (1, 2, 3)]
    for c in loads:
        c.start()
    greet_all(zyx)
    sends = []

    def go(c):
        c.start()
        sends.append(c)
        return c

    to2 = go(remote(pair_ref, pr.at[2], p_send.at[0], p_recv.at[0], {"dp": dp ^ 2}))
    to1 = go(remote(pair_ref, pr.at[1], p_send.at[1], p_recv.at[1], {"dp": dp ^ 1}))
    toz = {d: go(remote(pair_ref, pz.at[4 - d], p_send.at[1 + d], p_recv.at[5 - d], {"section": (z + d) % 4}))
           for d in (1, 3, 2)}
    to2.wait_recv()
    to3 = go(remote(pr.at[2], pr.at[3], f_send, f_recv, {"dp": dp ^ 1}))
    to1.wait_recv()
    for c in loads[:6]:
        c.wait()
    to3.wait_recv()

    def wgrad(j, _):
        cols = pl.ds(pl.multiple_of(j * 512, 512), 512)
        acc = dg(pr[0], gq[0, :, cols], 0, 0)
        for s in (1, 2, 3):
            acc = acc + dg(pr[s], gq[s, :, cols], 0, 0)
        wq[cols] = acc.T.astype(BF).reshape(512, 2, 128)
        return 0

    lax.fori_loop(0, 4, wgrad, 0)

    def wrows(d):
        return wg_ref.at[pl.ds(pl.multiple_of(d * 2048, 2048), 2048)]

    g2 = go(remote(wq, wrows(dp), g_send.at[0], g_recv.at[0], {"dp": dp ^ 2}))
    g1 = go(remote(wq, wrows(dp), g_send.at[1], g_recv.at[1], {"dp": dp ^ 1}))
    mine = pltpu.make_async_copy(wq, wrows(dp), o_sem.at[0])
    mine.start()
    for c in loads[6:]:
        c.wait()
    for k in (1, 2, 3):
        pltpu.make_async_copy(pz.at[k], pz.at[k], p_recv.at[1 + k]).wait()

    for h in range(2):
        def tile_part(j, _, h=h):
            wc = pl.ds(pl.multiple_of(h * 1024 + j * 512, 512), 512)
            cols = pl.ds(pl.multiple_of(j * 512, 512), 512)
            acc = dg(pz[0], wv[0, wc].reshape(512, 256), 1, 1)
            for k in (1, 2, 3):
                acc = acc + dg(pz[k], wv[k, wc].reshape(512, 256), 1, 1)
            t = acc.astype(BF)
            for k in range(4):
                tp[h, :, :, k, :, cols] = t[k * 128:(k + 1) * 128].reshape(4, 2, 16, 512)
            return 0

        lax.fori_loop(0, 2, tile_part, 0)
        for d in (1, 3, 2):
            t = (y + d) % 4
            go(remote(tp.at[h, t], rs.at[h, 3 - d], y_send.at[h, d - 1], y_recv.at[h, 3 - d], {"tensor": t * 2 + x}))

    for h in range(2):
        for s in range(3):
            pltpu.make_async_copy(rs.at[h, s], rs.at[h, s], y_recv.at[h, s]).wait()
        for e in range(2):
            tot = tp[h, y, e].astype(F32)
            for s in range(3):
                tot = tot + rs[h, s, e].astype(F32)
            own[h, e] = tot
        xs[h] = own[h, 1 - x].astype(BF)
        go(remote(xs.at[h], xr.at[h], x_send.at[h], x_recv.at[h], {"tensor": y * 2 + (1 - x)}))

    outs = [mine]
    for h in range(2):
        pltpu.make_async_copy(xr.at[h], xr.at[h], x_recv.at[h]).wait()
        zs[h] = (own[h, x] + xr[h].astype(F32)).astype(BF)
        cols = pl.ds(pl.multiple_of(z * 2048 + h * 1024, 1024), 1024)
        for d in (1, 3, 2):
            t = (z + d) % 4
            go(remote(zs.at[h, t], tg_ref.at[:, cols], z_send.at[h, d - 1], z_recv.at[h, 3 - d], {"section": t}))
        c = pltpu.make_async_copy(zs.at[h, z], tg_ref.at[:, cols], o_sem.at[1 + h])
        c.start()
        outs.append(c)

    g2.wait_recv()
    g3 = go(remote(wrows(dp ^ 2), wrows(dp ^ 2), h_send, h_recv, {"dp": dp ^ 1}))
    g1.wait_recv()
    g3.wait_recv()
    for h in range(2):
        for d in (1, 2, 3):
            s = (z + d) % 4
            v = tg_ref.at[:, pl.ds(pl.multiple_of(s * 2048 + h * 1024, 1024), 1024)]
            pltpu.make_async_copy(v, v, z_recv.at[h, d - 1]).wait()
    for c in outs:
        c.wait()
    for c in sends:
        c.wait_send()


def tail(pair, others, every_tile, wz, weight):
    hbm = pl.BlockSpec(memory_space=pl.ANY)
    dma = pltpu.SemaphoreType.DMA
    return pl.pallas_call(
        tail_kernel,
        in_specs=[hbm] * 5,
        out_specs=[hbm] * 2,
        out_shape=[jax.ShapeDtypeStruct((16, 8192), BF), jax.ShapeDtypeStruct((8192, 2, 128), BF)],
        scratch_shapes=[
            pltpu.VMEM((4, 512, 256), BF), pltpu.VMEM((4, 512, 256), BF), pltpu.VMEM((4, 512, 2048), BF),
            pltpu.VMEM((4, 2048, 2, 128), BF), pltpu.VMEM((2048, 2, 128), BF),
            pltpu.VMEM((2, 4, 2, 4, 16, 1024), BF), pltpu.VMEM((2, 3, 2, 4, 16, 1024), BF),
            pltpu.VMEM((2, 2, 4, 16, 1024), F32), pltpu.VMEM((2, 4, 16, 1024), BF),
            pltpu.VMEM((2, 4, 16, 1024), BF), pltpu.VMEM((2, 4, 16, 1024), BF),
            dma((10,)), dma((5,)), dma((5,)), dma, dma, dma((2,)), dma((2,)), dma, dma,
            dma((2, 3)), dma((2, 3)), dma((2,)), dma((2,)), dma((2, 3)), dma((2, 3)), dma((3,))],
        compiler_params=pltpu.CompilerParams(
            vmem_limit_bytes=60 * 2**20, collective_id=2, has_side_effects=True),
    )(pair, others, every_tile, wz, weight)


def local(queries, grad_out, tiles, key_value_matrix, gate, tile_count):
    packed = key_value_matrix.reshape(8192, 2, 128)
    every_tile = all_gather_tiles(tiles)
    kv = jnp.dot(every_tile, packed.reshape(8192, 256), preferred_element_type=F32).astype(BF)
    query_grad, pair, others, wz = attention(
        queries[0, 0], grad_out[0, 0], kv, tile_count, jnp.tanh(gate), tiles, every_tile, packed
    )
    tile_grad, weight_gradient = tail(pair, others, every_tile, wz, packed)
    return (query_grad[None, None], tile_grad[None], weight_gradient.reshape(1, 8192, 1, 2, 128))


def solution(mesh):
    return jax.shard_map(
        local,
        mesh=mesh,
        in_specs=(
            P("section", "dp", None, "tensor"),
            P("section", "dp", None, "tensor"),
            P("dp", ("section", "tensor"), None),
            P("section", None, "tensor", None, None),
            P("section"),
            P("dp"),
        ),
        out_specs=(
            P("section", "dp", None, "tensor"),
            P("dp", ("section", "tensor"), None),
            P("section", None, "tensor", None, None),
        ),
        check_vma=False,
    )
```

```python
import functools
import heapq

import jax
import jax.numpy as jnp
from jax import lax
from jax.experimental import pallas as pl
from jax.experimental.pallas import tpu as pltpu
from jax.sharding import PartitionSpec as P

F32, BF = jnp.float32, jnp.bfloat16
SC = 128 ** -0.5
LOG2E = 1.4426950408889634


def dg(a, b, ca, cb):
    return lax.dot_general(a, b, (((ca,), (cb,)), ((), ())), preferred_element_type=F32)

MESH = pl.DeviceIdType.MESH
SIZES = {"z": 4, "y": 4, "x": 2}
AX = "zyx"

def gather_plan(parts, latency=0.3):
    def dirs(a):
        return (1,) if SIZES[a] == 2 else (1, -1)
    def shift(u, a, s):
        u = list(u); n = AX.index(a); u[n] = (u[n] - s) % SIZES[a]
        return tuple(u)
    def sends_of(p, u, via):
        order, _, flip = parts[p]
        out = []
        if via is not None:
            a, s = via
            k = order.index(a)
            if SIZES[a] == 4 and u[AX.index(a)] in (1, 3):
                d = -1 if u[AX.index(a)] == 1 else 1
                par = (sum(u[AX.index(b)] for b in order[:k]) + flip) % 2
                if (d == 1) == (par == 0):
                    out.append((p, u, a, d))
            rest = order[k + 1:]
        else:
            rest = order
        for a in rest:
            for d in dirs(a):
                out.append((p, u, a, d))
        return out
    free = {}
    heap = []
    cnt = 0
    def push(t, sends):
        nonlocal cnt
        for (p, u, a, d) in sends:
            t0 = max(t, free.get((a, d), 0.0))
            t1 = t0 + parts[p][1]
            free[(a, d)] = t1
            cnt += 1
            heapq.heappush(heap, (t1 + latency, cnt, p, shift(u, a, d), (a, d)))
    init = [s for p in range(len(parts)) for s in sends_of(p, (0, 0, 0), None)]
    push(0.0, init)
    events, last = [], 0.0
    while heap:
        t, _, p, u, via = heapq.heappop(heap)
        s = sends_of(p, u, via)
        events.append((t, p, u, s))
        push(t, s)
        last = t
    for p in range(len(parts)):
        got = sorted(u for _, q, u, _ in events if q == p)
        full = 1
        for a in parts[p][0]:
            full *= SIZES[a]
        assert len(got) == len(set(got)) == full - 1
    return init, events, last, dict(free)

def place():
    z = lax.axis_index("section"); t = lax.axis_index("tensor")
    return z, t // 2, t % 2

def neighbour(zyx, a, d):
    z, y, x = zyx
    if a == "z":
        return {"section": (z + d) % 4}
    if a == "y":
        return {"tensor": ((y + d) % 4) * 2 + x}
    return {"tensor": y * 2 + (1 - x)}

def uidx(u):
    return u[0] * 8 + u[1] * 2 + u[2]

def row_of(zyx, u):
    z, y, x = zyx
    return ((z + u[0]) % 4) * 8 + ((y + u[1]) % 4) * 2 + (x + u[2]) % 2

def greet(zyx):
    bar = pltpu.get_barrier_semaphore()
    ns = [("x", 1), ("y", 1), ("y", -1), ("z", 1), ("z", -1)]
    for a, d in ns:
        pl.semaphore_signal(bar, inc=1, device_id=neighbour(zyx, a, d), device_id_type=MESH)
    pl.semaphore_wait(bar, len(ns))

PARTS = {4: [("xyz", 0.6875, 0), ("xzy", 0.6875, 0), ("yzx", 0.3125, 0), ("zyx", 0.3125, 1)]}
COLS = {4: [(0, 2816), (2816, 2816), (5632, 1280), (6912, 1280)]}

def ag_kernel(np_, tiles_ref, w_ref, kv_ref, out_ref, buf, raw, wide, acc, send_sem, recv_sem, loc_sem):
    zyx = place()
    dp = lax.axis_index("dp")
    init, events, _, _ = gather_plan(PARTS[np_])
    cols = COLS[np_]
    mine = row_of(zyx, (0, 0, 0))
    loc = pltpu.make_async_copy(tiles_ref.at[0], buf.at[pl.ds(pl.multiple_of(mine * 16, 16), 16)], loc_sem.at[0])
    loc.start()
    load_w = pltpu.make_async_copy(w_ref, raw, loc_sem.at[1])
    load_w.start()
    greet(zyx)
    started = []

    def view(ref, p, u):
        return ref.at[pl.ds(pl.multiple_of(row_of(zyx, u) * 16, 16), 16), pl.ds(*cols[p])]

    def start(p, u, a, d):
        n = AX.index(a)
        v = list(u)
        v[n] = (v[n] - d) % SIZES[a]
        src = tiles_ref.at[0, :, pl.ds(*cols[p])] if u == (0, 0, 0) else view(buf, p, u)
        c = pltpu.make_async_remote_copy(
            src_ref=src, dst_ref=view(buf, p, u),
            send_sem=send_sem.at[len(started)], recv_sem=recv_sem.at[p * 32 + uidx(v)],
            device_id=neighbour(zyx, a, d), device_id_type=MESH)
        c.start()
        started.append(c)

    def wait(p, u):
        v = view(buf, p, u)
        pltpu.make_async_copy(v, v, recv_sem.at[p * 32 + uidx(u)]).wait()

    for s in init:
        start(*s)
    done = 0
    for n, (_, p, u, sends) in enumerate(events):
        wait(p, u)
        for s in sends:
            start(*s)
        if n % 12 == 5 and done < 8:
            if done == 0:
                load_w.wait()
            rows = pl.ds(done * 1024, 1024)
            wide[rows] = raw[rows].reshape(1024, 256)
            done += 1
    assert done == 8
    loc.wait()
    outs = []
    for k in range(2):
        c = pltpu.make_async_copy(
            buf.at[:, pl.ds(pl.multiple_of((dp ^ k) * 2048, 2048), 2048)], out_ref.at[k], loc_sem.at[2 + k])
        c.start()
        outs.append(c)
    acc[...] = jnp.zeros_like(acc)

    def project(j, _):
        at = pl.ds(pl.multiple_of(j * 1024, 1024), 1024)
        acc[...] += dg(buf[:, at], wide[at], 1, 0)
        return 0

    lax.fori_loop(0, 8, project, 0)
    kv_ref[...] = acc[...].astype(BF)
    for c in started:
        c.wait_send()
    for c in outs:
        c.wait()


def nsends(np_):
    init, events, _, _ = gather_plan(PARTS[np_])
    return len(init) + sum(len(e[3]) for e in events)


def gather_and_project(tiles, weight, np_=4, cid=0):
    dma = pltpu.SemaphoreType.DMA
    hbm = pl.BlockSpec(memory_space=pl.ANY)
    return pl.pallas_call(
        functools.partial(ag_kernel, np_),
        in_specs=[hbm, hbm],
        out_specs=[pl.BlockSpec(memory_space=pltpu.VMEM), hbm],
        out_shape=[jax.ShapeDtypeStruct((512, 256), BF), jax.ShapeDtypeStruct((2, 512, 2048), BF)],
        scratch_shapes=[
            pltpu.VMEM((512, 8192), BF), pltpu.VMEM((8192, 2, 128), BF), pltpu.VMEM((8192, 256), BF),
            pltpu.VMEM((512, 256), F32), dma((nsends(np_),)), dma((np_ * 32,)), dma((4,))],
        compiler_params=pltpu.CompilerParams(
            vmem_limit_bytes=60 * 2**20, collective_id=cid, has_side_effects=True),
    )(tiles, weight)


def attention_rows(lay, sub, f, cnt, q_ref, g_ref, kv_ref, dq_ref, ka, va, opt=""):
    k = kv_ref[:, :128]; v = kv_ref[:, 128:]
    J = k.shape[0]; R = q_ref.shape[0]; H = J // 2
    ax = 0 if lay == "T" else 1
    valid = lax.broadcasted_iota(jnp.int32, (H, 1) if ax == 0 else (1, H), ax) + H < cnt
    items = [(h, r) for r in range(R // sub) for h in range(8)]
    def first(it):
        h, r = it
        rs = pl.ds(r * sub, sub); c = pl.ds(h * 128, 128)
        q = q_ref[rs, c]; g = (f * g_ref[rs, c].astype(F32)).astype(BF)
        if lay == "T": return q, g, dg(k, q, 1, 1), dg(v, g, 1, 1)
        return q, g, dg(q, k, 1, 1), dg(g, v, 1, 1)
    def mid(q, g, s, dp):
        if ax == 0: s = jnp.concatenate([s[:H], jnp.where(valid, s[H:], -jnp.inf)], axis=0)
        else: s = jnp.concatenate([s[:, :H], jnp.where(valid, s[:, H:], -jnp.inf)], axis=1)
        m = jnp.max(s, axis=ax, keepdims=True)
        e = jnp.exp2((s - m) * (SC * LOG2E))
        inv = 1.0 / jnp.sum(e, axis=ax, keepdims=True)
        delta = jnp.sum(e * dp, axis=ax, keepdims=True) * inv
        ph = (e * inv).astype(BF)
        ds = ((e * (inv * SC)) * (dp - delta)).astype(BF)
        return ds, ph
    def last(it, q, g, ds, ph):
        h, r = it
        o = (pl.ds(r * sub, sub), pl.ds(h * 128, 128))
        if lay == "T":
            dq_ref[o] = dg(k, ds, 0, 0).T.astype(BF)
            ka[...] += dg(ds, q, 1, 0); va[...] += dg(ph, g, 1, 0)
        else:
            dq_ref[o] = dg(ds, k, 1, 0).astype(BF)
            ka[...] += dg(q, ds, 0, 0); va[...] += dg(g, ph, 0, 0)
    nxt = first(items[0]); prev = None
    for n, it in enumerate(items):
        cur = nxt
        if n + 1 < len(items): nxt = first(items[n + 1])
        if prev is not None: last(*prev)
        b = mid(*cur)
        prev = (it, cur[0], cur[1], *b)
    last(*prev)


def background_plan(steps, unit_us=4.0, start_us=9.0, step_us=3.5):
    parts = [("zy", 1.0, 0), ("yz", 1.0, 1)]
    init, events, _, _ = gather_plan(parts, latency=0.7)
    per_step = [[] for _ in range(steps)]
    for t, p, u, sends in events:
        n = int((start_us + t * unit_us) / step_us) + 1
        per_step[min(n, steps - 1)].append((p, u, sends))
    return init, per_step


def count_sends(init, per_step):
    return len(init) + sum(len(e[2]) for b in per_step for e in b)


def greet_all(zyx):
    z, y, x = zyx
    dp = lax.axis_index("dp")
    peers = [{"section": (z + d) % 4} for d in (1, 2, 3)]
    peers += [{"tensor": ((y + d) % 4) * 2 + x} for d in (1, 2, 3)]
    peers += [{"tensor": y * 2 + (1 - x)}]
    peers += [{"dp": dp ^ k} for k in (1, 2, 3)]
    bar = pltpu.get_barrier_semaphore()
    for d in peers:
        pl.semaphore_signal(bar, inc=1, device_id=d, device_id_type=MESH)
    pl.semaphore_wait(bar, len(peers))


def attention_kernel(steps, cnt_ref, fac_ref, q_ref, g_ref, kv_ref, tiles_ref, all_ref, w_ref,
                     dq_ref, pair_ref, others_ref, wz_ref, ka, va,
                     send_sem, recv_sem, swap_send, swap_recv, e_send, e_recv, w_send, w_recv, c_send, c_recv, x_send, x_recv):
    i = pl.program_id(0)
    zyx = place()
    z, y, x = zyx
    dp = lax.axis_index("dp")
    core = dp % 2
    init, per_step = background_plan(steps)
    started = []

    def rows(u):
        return pl.ds(pl.multiple_of(row_of(zyx, u) * 16, 16), 16)

    def pair_rows(u):
        at = ((z + u[0]) % 4) * 8 + ((y + u[1]) % 4) * 2
        return pl.ds(pl.multiple_of(at * 16, 32), 32)

    def quarter(d):
        return pl.ds(pl.multiple_of(d * 2048, 2048), 2048)

    def part_copy(p, u, a, d, at=None):
        if at is None:
            at = len(started)
            started.append((p, u, a, d, at))
        n = AX.index(a)
        v = list(u)
        v[n] = (v[n] - d) % SIZES[a]
        c = pltpu.make_async_remote_copy(
            src_ref=others_ref.at[p, pair_rows(u)], dst_ref=others_ref.at[p, pair_rows(u)],
            send_sem=send_sem.at[at], recv_sem=recv_sem.at[p * 32 + uidx(v)],
            device_id=neighbour(zyx, a, d), device_id_type=MESH)
        return c

    def landed(ref, sem):
        pltpu.make_async_copy(ref, ref, sem).wait()

    def swap(p):
        return pltpu.make_async_remote_copy(
            src_ref=tiles_ref.at[0, :, quarter(dp ^ (2 + p))], dst_ref=others_ref.at[p, rows((0, 0, 0))],
            send_sem=swap_send.at[p], recv_sem=swap_recv.at[p], device_id={"dp": dp ^ (2 + p)}, device_id_type=MESH)

    def across(p, far=0):
        u = others_ref.at[p, rows((0, 0, far))]
        return pltpu.make_async_remote_copy(
            src_ref=u, dst_ref=u, send_sem=e_send.at[p], recv_sem=e_recv.at[p],
            device_id=neighbour(zyx, "x", 1), device_id_type=MESH)

    def w_copy(h, d):
        t = ((z, y)[h] + d) % 4
        dev = {"section": t} if h == 0 else {"tensor": t * 2 + x}
        return pltpu.make_async_remote_copy(
            src_ref=w_ref.at[pl.ds(pl.multiple_of(h * 4096 + t * 1024 + core * 512, 512), 512)],
            dst_ref=wz_ref.at[h, 4 - d, pl.ds(pl.multiple_of(core * 512, 512), 512)],
            send_sem=w_send.at[h, d - 1], recv_sem=w_recv.at[h, 3 - d], device_id=dev, device_id_type=MESH)

    def half(h, k, c):
        return wz_ref.at[h, k, pl.ds(pl.multiple_of(c * 512, 512), 512)]

    def c_copy(h, k):
        return pltpu.make_async_remote_copy(
            src_ref=half(h, k, core), dst_ref=half(h, k, core), send_sem=c_send.at[h, k - 1],
            recv_sem=c_recv.at[h, k - 1], device_id={"dp": dp ^ 1}, device_id_type=MESH)

    def x_copy():
        return pltpu.make_async_remote_copy(
            src_ref=all_ref.at[1], dst_ref=others_ref.at[2],
            send_sem=x_send, recv_sem=x_recv, device_id={"dp": dp ^ 1}, device_id_type=MESH)

    @pl.when(i == 0)
    def _():
        ka[...] = jnp.zeros_like(ka)
        va[...] = jnp.zeros_like(va)
        greet_all(zyx)
        for p in (0, 1):
            swap(p).start()
        for d in (1, 3):
            for h in (0, 1):
                w_copy(h, d).start()
        x_copy().start()

    for n in range(1, steps):
        def batch(n=n):
            if n == 1:
                for p in (0, 1):
                    landed(others_ref.at[p, rows((0, 0, 0))], swap_recv.at[p])
                    across(p).start()
            if n == 2:
                for p in (0, 1):
                    landed(others_ref.at[p, rows((0, 0, 1))], e_recv.at[p])
                for s in init:
                    part_copy(*s).start()
            for p, u, sends in per_step[n]:
                landed(others_ref.at[p, pair_rows(u)], recv_sem.at[p * 32 + uidx(u)])
                for s in sends:
                    part_copy(*s).start()
            if n == 8:
                for h in (0, 1):
                    w_copy(h, 2).start()
            if n == steps - 1:
                for k in (1, 3, 2):
                    for h in (0, 1):
                        landed(half(h, k, core), w_recv.at[h, k - 1])
                        c_copy(h, k).start()
        assert n >= 2 or not per_step[n]
        if n in (1, 2, 8, steps - 1) or per_step[n]:
            pl.when(i == n)(batch)

    attention_rows("L", q_ref.shape[0], fac_ref[0], cnt_ref[0], q_ref, g_ref, kv_ref, dq_ref, ka, va)

    @pl.when(i == steps - 1)
    def _():
        pair_ref[:, :128] = ka[...].T.astype(BF)
        pair_ref[:, 128:] = va[...].T.astype(BF)
        for s in started:
            part_copy(*s).wait_send()
        for p in (0, 1):
            swap(p).wait_send()
        for p in (0, 1):
            across(p).wait_send()
        for h in (0, 1):
            for d in (1, 2, 3):
                w_copy(h, d).wait_send()
            for k in (1, 2, 3):
                c_copy(h, k).wait_send()
                landed(half(h, k, 1 - core), c_recv.at[h, k - 1])
        x_copy().wait()


def attention(q, g, kv, cnt, fac, tiles, every_tile, weight, R=256):
    n = q.shape[0]
    steps = n // R
    hbm = pl.BlockSpec(memory_space=pl.ANY)
    dma = pltpu.SemaphoreType.DMA
    return pl.pallas_call(
        functools.partial(attention_kernel, steps),
        grid=(steps,),
        in_specs=[pl.BlockSpec(memory_space=pltpu.SMEM)] * 2 + [
            pl.BlockSpec((R, 1024), lambda i: (i, 0)),
            pl.BlockSpec((R, 1024), lambda i: (i, 0)),
            pl.BlockSpec((512, 256), lambda i: (0, 0)), hbm, hbm, hbm],
        out_specs=[pl.BlockSpec((R, 1024), lambda i: (i, 0)), pl.BlockSpec((512, 256), lambda i: (0, 0)), hbm, hbm],
        out_shape=[jax.ShapeDtypeStruct((n, 1024), BF), jax.ShapeDtypeStruct((512, 256), BF),
                   jax.ShapeDtypeStruct((3, 512, 2048), BF), jax.ShapeDtypeStruct((2, 4, 1024, 2, 128), BF)],
        scratch_shapes=[pltpu.VMEM((128, 512), F32)] * 2 + [
            dma((count_sends(*background_plan(steps)),)), dma((64,)), dma((2,)), dma((2,)), dma((2,)), dma((2,)),
            dma((2, 3)), dma((2, 3)), dma((2, 3)), dma((2, 3)), dma, dma],
        compiler_params=pltpu.CompilerParams(
            vmem_limit_bytes=60 * 2**20, dimension_semantics=("arbitrary",), collective_id=1, has_side_effects=True),
    )(cnt, fac, q, g, kv, tiles, every_tile, weight)


def tail_kernel(pair_ref, others_ref, all_ref, wz_ref, w_ref, tg_ref, wg_ref,
                pza, pzb, pr, gq, wv, wq, tp, rs, own, xs, xr, zs,
                l_sem, p_send, p_recv, s_send, s_recv, f_send, f_recv, g_send, g_recv, h_send, h_recv,
                y_send, y_recv, x_send, x_recv, z_send, z_recv, o_sem):
    zyx = place()
    z, y, x = zyx
    dp = lax.axis_index("dp")

    def remote(src, dst, ss, rs_, dev):
        return pltpu.make_async_remote_copy(
            src_ref=src, dst_ref=dst, send_sem=ss, recv_sem=rs_, device_id=dev, device_id_type=MESH)

    loads = [pltpu.make_async_copy(pair_ref, pr.at[0], l_sem.at[0]),
             pltpu.make_async_copy(all_ref.at[0], gq.at[0], l_sem.at[1]),
             pltpu.make_async_copy(others_ref.at[2], gq.at[1], l_sem.at[2]),
             pltpu.make_async_copy(others_ref.at[0], gq.at[2], l_sem.at[3]),
             pltpu.make_async_copy(others_ref.at[1], gq.at[3], l_sem.at[4])]
    for h in range(2):
        at = pl.multiple_of(h * 4096 + (z, y)[h] * 1024, 1024)
        loads.append(pltpu.make_async_copy(w_ref.at[pl.ds(at, 1024)], wv.at[h, 0], l_sem.at[5 + h * 4]))
        for k in (1, 2, 3):
            loads.append(pltpu.make_async_copy(wz_ref.at[h, k], wv.at[h, k], l_sem.at[5 + h * 4 + k]))
    for c in loads:
        c.start()
    greet_all(zyx)
    sends = []

    def go(c):
        c.start()
        sends.append(c)
        return c

    to2 = go(remote(pair_ref, pr.at[2], p_send.at[0], p_recv.at[0], {"dp": dp ^ 2}))
    to1 = go(remote(pair_ref, pr.at[1], p_send.at[1], p_recv.at[1], {"dp": dp ^ 1}))
    def peer(h, t):
        return {"section": t} if h == 0 else {"tensor": t * 2 + x}

    def part(ref, h, e):
        return ref.at[pl.ds(2 * e, 2)] if h == 0 else ref.at[:, pl.ds(2 * e, 2)]

    at = (z, y)
    pz = (pza, pzb)
    for e in range(2):
        for d in (1, 3, 2):
            for h in range(2):
                go(remote(part(pair_ref, h, e), pz[h].at[3 - d, e], s_send.at[h, d - 1, e], s_recv.at[h, 3 - d, e],
                          peer(h, (at[h] + d) % 4)))
    to2.wait_recv()
    to3 = go(remote(pr.at[2], pr.at[3], f_send, f_recv, {"dp": dp ^ 1}))
    to1.wait_recv()
    for c in loads[:5]:
        c.wait()
    to3.wait_recv()

    def wgrad(j, _):
        cols = pl.ds(pl.multiple_of(j * 512, 512), 512)
        acc = dg(pr[0].reshape(512, 256), gq[0, :, cols], 0, 0)
        for s in (1, 2, 3):
            acc = acc + dg(pr[s].reshape(512, 256), gq[s, :, cols], 0, 0)
        wq[cols] = acc.T.astype(BF).reshape(512, 2, 128)
        return 0

    lax.fori_loop(0, 4, wgrad, 0)

    def wrows(d):
        return wg_ref.at[pl.ds(pl.multiple_of(d * 2048, 2048), 2048)]

    g2 = go(remote(wq, wrows(dp), g_send.at[0], g_recv.at[0], {"dp": dp ^ 2}))
    g1 = go(remote(wq, wrows(dp), g_send.at[1], g_recv.at[1], {"dp": dp ^ 1}))
    mine = pltpu.make_async_copy(wq, wrows(dp), o_sem.at[0])
    mine.start()
    for c in loads[5:]:
        c.wait()
    for e in range(2):
        for h in range(2):
            for k in range(3):
                pltpu.make_async_copy(pz[h].at[k, e], pz[h].at[k, e], s_recv.at[h, k, e]).wait()

            def tile_part(j, _, h=h, e=e):
                cols = pl.ds(pl.multiple_of(j * 512, 512), 512)
                rows = part(pr.at[0], h, e)[...].reshape(256, 256)
                acc = dg(rows, wv[h, 0, cols].reshape(512, 256), 1, 1)
                for k in range(3):
                    acc = acc + dg(pz[h][k, e].reshape(256, 256), wv[h, k + 1, cols].reshape(512, 256), 1, 1)
                t = acc.astype(BF)
                for a in range(2 if h == 0 else 4):
                    for b in range(4 if h == 0 else 2):
                        n = (a * 4 + b) if h == 0 else (a * 2 + b)
                        block = t[n * 32:(n + 1) * 32].reshape(2, 16, 512)
                        if h == 0:
                            tp[h, e, b, :, a, :, cols] = block
                        else:
                            tp[h, e, a, :, b, :, cols] = block
                return 0

            lax.fori_loop(0, 2, tile_part, 0)
            for d in (1, 3, 2):
                t = (at[1 - h] + d) % 4
                go(remote(tp.at[h, e, t], rs.at[h, e, 3 - d], y_send.at[h, e, d - 1], y_recv.at[h, e, 3 - d],
                          peer(1 - h, t)))

    for e in range(2):
        for h in range(2):
            for s in range(3):
                pltpu.make_async_copy(rs.at[h, e, s], rs.at[h, e, s], y_recv.at[h, e, s]).wait()
            for f in range(2):
                tot = tp[h, e, at[1 - h], f].astype(F32)
                for s in range(3):
                    tot = tot + rs[h, e, s, f].astype(F32)
                own[h, e, f] = tot
            xs[h, e] = own[h, e, 1 - x].astype(BF)
            go(remote(xs.at[h, e], xr.at[h, e], x_send.at[h, e], x_recv.at[h, e], {"tensor": y * 2 + (1 - x)}))

    outs = [mine]
    for h in range(2):
        for e in range(2):
            pltpu.make_async_copy(xr.at[h, e], xr.at[h, e], x_recv.at[h, e]).wait()
            zs[h, pl.ds(2 * e, 2)] = (own[h, e, x] + xr[h, e].astype(F32)).astype(BF)
        cols = pl.ds(pl.multiple_of(h * 4096 + at[h] * 1024, 1024), 1024)
        for d in (1, 3, 2):
            t = (at[h] + d) % 4
            go(remote(zs.at[h, t], tg_ref.at[:, cols], z_send.at[h, d - 1], z_recv.at[h, 3 - d], peer(h, t)))
        c = pltpu.make_async_copy(zs.at[h, at[h]], tg_ref.at[:, cols], o_sem.at[1 + h])
        c.start()
        outs.append(c)

    g2.wait_recv()
    g3 = go(remote(wrows(dp ^ 2), wrows(dp ^ 2), h_send, h_recv, {"dp": dp ^ 1}))
    g1.wait_recv()
    g3.wait_recv()
    for h in range(2):
        for d in (1, 2, 3):
            s = (at[h] + d) % 4
            v = tg_ref.at[:, pl.ds(pl.multiple_of(h * 4096 + s * 1024, 1024), 1024)]
            pltpu.make_async_copy(v, v, z_recv.at[h, d - 1]).wait()
    for c in outs:
        c.wait()
    for c in sends:
        c.wait_send()


def tail(pair, others, every_tile, wz, weight):
    hbm = pl.BlockSpec(memory_space=pl.ANY)
    dma = pltpu.SemaphoreType.DMA
    return pl.pallas_call(
        tail_kernel,
        in_specs=[hbm] * 5,
        out_specs=[hbm] * 2,
        out_shape=[jax.ShapeDtypeStruct((16, 8192), BF), jax.ShapeDtypeStruct((8192, 2, 128), BF)],
        scratch_shapes=[
            pltpu.VMEM((3, 2, 2, 4, 32, 256), BF), pltpu.VMEM((3, 2, 4, 2, 32, 256), BF), pltpu.VMEM((4, 4, 4, 32, 256), BF), pltpu.VMEM((4, 512, 2048), BF),
            pltpu.VMEM((2, 4, 1024, 2, 128), BF), pltpu.VMEM((2048, 2, 128), BF),
            pltpu.VMEM((2, 2, 4, 2, 2, 16, 1024), BF), pltpu.VMEM((2, 2, 3, 2, 2, 16, 1024), BF),
            pltpu.VMEM((2, 2, 2, 2, 16, 1024), F32), pltpu.VMEM((2, 2, 2, 16, 1024), BF),
            pltpu.VMEM((2, 2, 2, 16, 1024), BF), pltpu.VMEM((2, 4, 16, 1024), BF),
            dma((13,)), dma((2,)), dma((2,)), dma((2, 3, 2)), dma((2, 3, 2)), dma, dma, dma((2,)), dma((2,)), dma, dma,
            dma((2, 2, 3)), dma((2, 2, 3)), dma((2, 2)), dma((2, 2)), dma((2, 3)), dma((2, 3)), dma((3,))],
        compiler_params=pltpu.CompilerParams(
            vmem_limit_bytes=50 * 2**20, collective_id=2, has_side_effects=True),
    )(pair, others, every_tile, wz, weight)


def local(queries, grad_out, tiles, key_value_matrix, gate, tile_count):
    packed = key_value_matrix.reshape(8192, 2, 128)
    kv, quarters = gather_and_project(tiles, packed)
    query_grad, pair, others, wz = attention(
        queries[0, 0], grad_out[0, 0], kv, tile_count, jnp.tanh(gate), tiles, quarters, packed
    )
    tile_grad, weight_gradient = tail(pair.reshape(4, 4, 32, 256), others, quarters, wz, packed)
    return (query_grad[None, None], tile_grad[None], weight_gradient.reshape(1, 8192, 1, 2, 128))


def solution(mesh):
    return jax.shard_map(
        local,
        mesh=mesh,
        in_specs=(
            P("section", "dp", None, "tensor"),
            P("section", "dp", None, "tensor"),
            P("dp", ("section", "tensor"), None),
            P("section", None, "tensor", None, None),
            P("section"),
            P("dp"),
        ),
        out_specs=(
            P("section", "dp", None, "tensor"),
            P("dp", ("section", "tensor"), None),
            P("section", None, "tensor", None, None),
        ),
        check_vma=False,
    )
```

```python
import functools
import heapq

import jax
import jax.numpy as jnp
from jax import lax
from jax.experimental import pallas as pl
from jax.experimental.pallas import tpu as pltpu
from jax.sharding import PartitionSpec as P

F32, BF = jnp.float32, jnp.bfloat16
SC = 128 ** -0.5
LOG2E = 1.4426950408889634


def dg(a, b, ca, cb):
    return lax.dot_general(a, b, (((ca,), (cb,)), ((), ())), preferred_element_type=F32)

MESH = pl.DeviceIdType.MESH
SIZES = {"z": 4, "y": 4, "x": 2}
AX = "zyx"

def gather_plan(parts, latency=0.3):
    def dirs(a):
        return (1,) if SIZES[a] == 2 else (1, -1)
    def shift(u, a, s):
        u = list(u); n = AX.index(a); u[n] = (u[n] - s) % SIZES[a]
        return tuple(u)
    def sends_of(p, u, via):
        order, _, flip = parts[p]
        out = []
        if via is not None:
            a, s = via
            k = order.index(a)
            if SIZES[a] == 4 and u[AX.index(a)] in (1, 3):
                d = -1 if u[AX.index(a)] == 1 else 1
                par = (sum(u[AX.index(b)] for b in order[:k]) + flip) % 2
                if (d == 1) == (par == 0):
                    out.append((p, u, a, d))
            rest = order[k + 1:]
        else:
            rest = order
        for a in rest:
            for d in dirs(a):
                out.append((p, u, a, d))
        return out
    free = {}
    heap = []
    cnt = 0
    def push(t, sends):
        nonlocal cnt
        for (p, u, a, d) in sends:
            t0 = max(t, free.get((a, d), 0.0))
            t1 = t0 + parts[p][1]
            free[(a, d)] = t1
            cnt += 1
            heapq.heappush(heap, (t1 + latency, cnt, p, shift(u, a, d), (a, d)))
    init = [s for p in range(len(parts)) for s in sends_of(p, (0, 0, 0), None)]
    push(0.0, init)
    events, last = [], 0.0
    while heap:
        t, _, p, u, via = heapq.heappop(heap)
        s = sends_of(p, u, via)
        events.append((t, p, u, s))
        push(t, s)
        last = t
    for p in range(len(parts)):
        got = sorted(u for _, q, u, _ in events if q == p)
        full = 1
        for a in parts[p][0]:
            full *= SIZES[a]
        assert len(got) == len(set(got)) == full - 1
    return init, events, last, dict(free)

def place():
    z = lax.axis_index("section"); t = lax.axis_index("tensor")
    return z, t // 2, t % 2

def neighbour(zyx, a, d):
    z, y, x = zyx
    if a == "z":
        return {"section": (z + d) % 4}
    if a == "y":
        return {"tensor": ((y + d) % 4) * 2 + x}
    return {"tensor": y * 2 + (1 - x)}

def uidx(u):
    return u[0] * 8 + u[1] * 2 + u[2]

def row_of(zyx, u):
    z, y, x = zyx
    return ((z + u[0]) % 4) * 8 + ((y + u[1]) % 4) * 2 + (x + u[2]) % 2

def greet(zyx):
    bar = pltpu.get_barrier_semaphore()
    ns = [("x", 1), ("y", 1), ("y", -1), ("z", 1), ("z", -1)]
    for a, d in ns:
        pl.semaphore_signal(bar, inc=1, device_id=neighbour(zyx, a, d), device_id_type=MESH)
    pl.semaphore_wait(bar, len(ns))

PARTS = {4: [("xyz", 0.6875, 0), ("xzy", 0.6875, 0), ("yzx", 0.3125, 0), ("zyx", 0.3125, 1)]}
COLS = {4: [(0, 2816), (2816, 2816), (5632, 1280), (6912, 1280)]}

def ag_kernel(np_, tiles_ref, w_ref, kv_ref, out_ref, buf, raw, wide, acc, send_sem, recv_sem, loc_sem):
    zyx = place()
    dp = lax.axis_index("dp")
    init, events, _, _ = gather_plan(PARTS[np_])
    cols = COLS[np_]
    mine = row_of(zyx, (0, 0, 0))
    loc = pltpu.make_async_copy(tiles_ref.at[0], buf.at[pl.ds(pl.multiple_of(mine * 16, 16), 16)], loc_sem.at[0])
    loc.start()
    load_w = pltpu.make_async_copy(w_ref, raw, loc_sem.at[1])
    load_w.start()
    greet(zyx)
    started = []

    def view(ref, p, u):
        return ref.at[pl.ds(pl.multiple_of(row_of(zyx, u) * 16, 16), 16), pl.ds(*cols[p])]

    def start(p, u, a, d):
        n = AX.index(a)
        v = list(u)
        v[n] = (v[n] - d) % SIZES[a]
        src = tiles_ref.at[0, :, pl.ds(*cols[p])] if u == (0, 0, 0) else view(buf, p, u)
        c = pltpu.make_async_remote_copy(
            src_ref=src, dst_ref=view(buf, p, u),
            send_sem=send_sem.at[len(started)], recv_sem=recv_sem.at[p * 32 + uidx(v)],
            device_id=neighbour(zyx, a, d), device_id_type=MESH)
        c.start()
        started.append(c)

    def wait(p, u):
        v = view(buf, p, u)
        pltpu.make_async_copy(v, v, recv_sem.at[p * 32 + uidx(u)]).wait()

    for s in init:
        start(*s)
    done = 0
    for n, (_, p, u, sends) in enumerate(events):
        wait(p, u)
        for s in sends:
            start(*s)
        if n % 12 == 5 and done < 8:
            if done == 0:
                load_w.wait()
            rows = pl.ds(done * 1024, 1024)
            wide[rows] = raw[rows].reshape(1024, 256)
            done += 1
    assert done == 8
    loc.wait()
    outs = []
    for k in range(2):
        c = pltpu.make_async_copy(
            buf.at[:, pl.ds(pl.multiple_of((dp ^ k) * 2048, 2048), 2048)], out_ref.at[k], loc_sem.at[2 + k])
        c.start()
        outs.append(c)
    acc[...] = jnp.zeros_like(acc)

    def project(j, _):
        at = pl.ds(pl.multiple_of(j * 1024, 1024), 1024)
        acc[...] += dg(buf[:, at], wide[at], 1, 0)
        return 0

    lax.fori_loop(0, 8, project, 0)
    kv_ref[...] = acc[...].astype(BF)
    for c in started:
        c.wait_send()
    for c in outs:
        c.wait()


def nsends(np_):
    init, events, _, _ = gather_plan(PARTS[np_])
    return len(init) + sum(len(e[3]) for e in events)


def gather_and_project(tiles, weight, np_=4, cid=0):
    dma = pltpu.SemaphoreType.DMA
    hbm = pl.BlockSpec(memory_space=pl.ANY)
    return pl.pallas_call(
        functools.partial(ag_kernel, np_),
        in_specs=[hbm, hbm],
        out_specs=[pl.BlockSpec(memory_space=pltpu.VMEM), hbm],
        out_shape=[jax.ShapeDtypeStruct((512, 256), BF), jax.ShapeDtypeStruct((2, 512, 2048), BF)],
        scratch_shapes=[
            pltpu.VMEM((512, 8192), BF), pltpu.VMEM((8192, 2, 128), BF), pltpu.VMEM((8192, 256), BF),
            pltpu.VMEM((512, 256), F32), dma((nsends(np_),)), dma((np_ * 32,)), dma((4,))],
        compiler_params=pltpu.CompilerParams(
            vmem_limit_bytes=60 * 2**20, collective_id=cid, has_side_effects=True),
    )(tiles, weight)


def attention_rows(lay, sub, f, cnt, q_ref, g_ref, kv_ref, dq_ref, ka, va, opt=""):
    k = kv_ref[:, :128]; v = kv_ref[:, 128:]
    J = k.shape[0]; R = q_ref.shape[0]; H = J // 2
    ax = 0 if lay == "T" else 1
    valid = lax.broadcasted_iota(jnp.int32, (H, 1) if ax == 0 else (1, H), ax) + H < cnt
    items = [(h, r) for r in range(R // sub) for h in range(8)]
    def first(it):
        h, r = it
        rs = pl.ds(r * sub, sub); c = pl.ds(h * 128, 128)
        q = q_ref[rs, c]; g = (f * g_ref[rs, c].astype(F32)).astype(BF)
        if lay == "T": return q, g, dg(k, q, 1, 1), dg(v, g, 1, 1)
        return q, g, dg(q, k, 1, 1), dg(g, v, 1, 1)
    def mid(q, g, s, dp):
        if ax == 0: s = jnp.concatenate([s[:H], jnp.where(valid, s[H:], -jnp.inf)], axis=0)
        else: s = jnp.concatenate([s[:, :H], jnp.where(valid, s[:, H:], -jnp.inf)], axis=1)
        m = jnp.max(s, axis=ax, keepdims=True)
        e = jnp.exp2((s - m) * (SC * LOG2E))
        inv = 1.0 / jnp.sum(e, axis=ax, keepdims=True)
        delta = jnp.sum(e * dp, axis=ax, keepdims=True) * inv
        ph = (e * inv).astype(BF)
        ds = ((e * (inv * SC)) * (dp - delta)).astype(BF)
        return ds, ph
    def last(it, q, g, ds, ph):
        h, r = it
        o = (pl.ds(r * sub, sub), pl.ds(h * 128, 128))
        if lay == "T":
            dq_ref[o] = dg(k, ds, 0, 0).T.astype(BF)
            ka[...] += dg(ds, q, 1, 0); va[...] += dg(ph, g, 1, 0)
        else:
            dq_ref[o] = dg(ds, k, 1, 0).astype(BF)
            ka[...] += dg(q, ds, 0, 0); va[...] += dg(g, ph, 0, 0)
    nxt = first(items[0]); prev = None
    for n, it in enumerate(items):
        cur = nxt
        if n + 1 < len(items): nxt = first(items[n + 1])
        if prev is not None: last(*prev)
        b = mid(*cur)
        prev = (it, cur[0], cur[1], *b)
    last(*prev)


def background_plan(steps, unit_us=4.0, start_us=12.0, step_us=3.5):
    parts = [("zy", 1.0, 0), ("yz", 1.0, 1)]
    init, events, _, _ = gather_plan(parts, latency=0.7)
    per_step = [[] for _ in range(steps)]
    for t, p, u, sends in events:
        n = int((start_us + t * unit_us) / step_us) + 1
        per_step[min(n, steps - 1)].append((p, u, sends))
    return init, per_step


def count_sends(init, per_step):
    return len(init) + sum(len(e[2]) for b in per_step for e in b)


def hello_all(zyx):
    z, y, x = zyx
    dp = lax.axis_index("dp")
    peers = [{"section": (z + d) % 4} for d in (1, 2, 3)]
    peers += [{"tensor": ((y + d) % 4) * 2 + x} for d in (1, 2, 3)]
    peers += [{"tensor": y * 2 + (1 - x)}]
    peers += [{"dp": dp ^ k} for k in (1, 2, 3)]
    for d in peers:
        pl.semaphore_signal(pltpu.get_barrier_semaphore(), inc=1, device_id=d, device_id_type=MESH)


def all_said_hello():
    pl.semaphore_wait(pltpu.get_barrier_semaphore(), 10)


def attention_kernel(steps, cnt_ref, fac_ref, q_ref, g_ref, kv_ref, tiles_ref, all_ref, w_ref,
                     dq_ref, pair_ref, others_ref, wz_ref, ka, va,
                     send_sem, recv_sem, swap_send, swap_recv, e_send, e_recv, w_send, w_recv, c_send, c_recv, x_send, x_recv):
    i = pl.program_id(0)
    zyx = place()
    z, y, x = zyx
    dp = lax.axis_index("dp")
    core = dp % 2
    init, per_step = background_plan(steps)
    started = []

    def rows(u):
        return pl.ds(pl.multiple_of(row_of(zyx, u) * 16, 16), 16)

    def pair_rows(u):
        at = ((z + u[0]) % 4) * 8 + ((y + u[1]) % 4) * 2
        return pl.ds(pl.multiple_of(at * 16, 32), 32)

    def quarter(d):
        return pl.ds(pl.multiple_of(d * 2048, 2048), 2048)

    def part_copy(p, u, a, d, at=None):
        if at is None:
            at = len(started)
            started.append((p, u, a, d, at))
        n = AX.index(a)
        v = list(u)
        v[n] = (v[n] - d) % SIZES[a]
        c = pltpu.make_async_remote_copy(
            src_ref=others_ref.at[p, pair_rows(u)], dst_ref=others_ref.at[p, pair_rows(u)],
            send_sem=send_sem.at[at], recv_sem=recv_sem.at[p * 32 + uidx(v)],
            device_id=neighbour(zyx, a, d), device_id_type=MESH)
        return c

    def landed(ref, sem):
        pltpu.make_async_copy(ref, ref, sem).wait()

    def swap(p):
        return pltpu.make_async_remote_copy(
            src_ref=tiles_ref.at[0, :, quarter(dp ^ (2 + p))], dst_ref=others_ref.at[p, rows((0, 0, 0))],
            send_sem=swap_send.at[p], recv_sem=swap_recv.at[p], device_id={"dp": dp ^ (2 + p)}, device_id_type=MESH)

    def across(p, far=0):
        u = others_ref.at[p, rows((0, 0, far))]
        return pltpu.make_async_remote_copy(
            src_ref=u, dst_ref=u, send_sem=e_send.at[p], recv_sem=e_recv.at[p],
            device_id=neighbour(zyx, "x", 1), device_id_type=MESH)

    def w_copy(h, d):
        t = ((z, y)[h] + d) % 4
        dev = {"section": t} if h == 0 else {"tensor": t * 2 + x}
        return pltpu.make_async_remote_copy(
            src_ref=w_ref.at[pl.ds(pl.multiple_of(h * 4096 + t * 1024 + core * 512, 512), 512)],
            dst_ref=wz_ref.at[h, 4 - d, pl.ds(pl.multiple_of(core * 512, 512), 512)],
            send_sem=w_send.at[h, d - 1], recv_sem=w_recv.at[h, 3 - d], device_id=dev, device_id_type=MESH)

    def half(h, k, c):
        return wz_ref.at[h, k, pl.ds(pl.multiple_of(c * 512, 512), 512)]

    def c_copy(h, k):
        return pltpu.make_async_remote_copy(
            src_ref=half(h, k, core), dst_ref=half(h, k, core), send_sem=c_send.at[h, k - 1],
            recv_sem=c_recv.at[h, k - 1], device_id={"dp": dp ^ 1}, device_id_type=MESH)

    def x_copy():
        return pltpu.make_async_remote_copy(
            src_ref=all_ref.at[1], dst_ref=others_ref.at[2],
            send_sem=x_send, recv_sem=x_recv, device_id={"dp": dp ^ 1}, device_id_type=MESH)

    @pl.when(i == 0)
    def _():
        ka[...] = jnp.zeros_like(ka)
        va[...] = jnp.zeros_like(va)
        hello_all(zyx)

    for n in range(1, steps):
        def batch(n=n):
            if n == 1:
                all_said_hello()
                for p in (0, 1):
                    swap(p).start()
                for d in (1, 3):
                    for h in (0, 1):
                        w_copy(h, d).start()
                x_copy().start()
            if n == 2:
                for p in (0, 1):
                    landed(others_ref.at[p, rows((0, 0, 0))], swap_recv.at[p])
                    across(p).start()
            if n == 3:
                for p in (0, 1):
                    landed(others_ref.at[p, rows((0, 0, 1))], e_recv.at[p])
                for s in init:
                    part_copy(*s).start()
            for p, u, sends in per_step[n]:
                landed(others_ref.at[p, pair_rows(u)], recv_sem.at[p * 32 + uidx(u)])
                for s in sends:
                    part_copy(*s).start()
            if n == 9:
                for h in (0, 1):
                    w_copy(h, 2).start()
            if n == steps - 1:
                for k in (1, 3, 2):
                    for h in (0, 1):
                        landed(half(h, k, core), w_recv.at[h, k - 1])
                        c_copy(h, k).start()
        assert n >= 4 or not per_step[n]
        if n in (1, 2, 3, 9, steps - 1) or per_step[n]:
            pl.when(i == n)(batch)

    attention_rows("L", q_ref.shape[0], fac_ref[0], cnt_ref[0], q_ref, g_ref, kv_ref, dq_ref, ka, va)

    @pl.when(i == steps - 1)
    def _():
        pair_ref[:, :128] = ka[...].T.astype(BF)
        pair_ref[:, 128:] = va[...].T.astype(BF)
        for s in started:
            part_copy(*s).wait_send()
        for p in (0, 1):
            swap(p).wait_send()
        for p in (0, 1):
            across(p).wait_send()
        for h in (0, 1):
            for d in (1, 2, 3):
                w_copy(h, d).wait_send()
            for k in (1, 2, 3):
                c_copy(h, k).wait_send()
                landed(half(h, k, 1 - core), c_recv.at[h, k - 1])
        x_copy().wait()


def attention(q, g, kv, cnt, fac, tiles, every_tile, weight, R=256):
    n = q.shape[0]
    steps = n // R
    hbm = pl.BlockSpec(memory_space=pl.ANY)
    dma = pltpu.SemaphoreType.DMA
    return pl.pallas_call(
        functools.partial(attention_kernel, steps),
        grid=(steps,),
        in_specs=[pl.BlockSpec(memory_space=pltpu.SMEM)] * 2 + [
            pl.BlockSpec((R, 1024), lambda i: (i, 0)),
            pl.BlockSpec((R, 1024), lambda i: (i, 0)),
            pl.BlockSpec((512, 256), lambda i: (0, 0)), hbm, hbm, hbm],
        out_specs=[pl.BlockSpec((R, 1024), lambda i: (i, 0)), pl.BlockSpec((512, 256), lambda i: (0, 0)), hbm, hbm],
        out_shape=[jax.ShapeDtypeStruct((n, 1024), BF), jax.ShapeDtypeStruct((512, 256), BF),
                   jax.ShapeDtypeStruct((3, 512, 2048), BF), jax.ShapeDtypeStruct((2, 4, 1024, 2, 128), BF)],
        scratch_shapes=[pltpu.VMEM((128, 512), F32)] * 2 + [
            dma((count_sends(*background_plan(steps)),)), dma((64,)), dma((2,)), dma((2,)), dma((2,)), dma((2,)),
            dma((2, 3)), dma((2, 3)), dma((2, 3)), dma((2, 3)), dma, dma],
        compiler_params=pltpu.CompilerParams(
            vmem_limit_bytes=60 * 2**20, dimension_semantics=("arbitrary",), collective_id=1, has_side_effects=True),
    )(cnt, fac, q, g, kv, tiles, every_tile, weight)


def tail_kernel(pair_ref, others_ref, all_ref, wz_ref, w_ref, tg_ref, wg_ref,
                pza, pzb, pr, gq, wv, wq, tp, rs, own, xs, xr, zs,
                l_sem, p_send, p_recv, s_send, s_recv, f_send, f_recv, g_send, g_recv, h_send, h_recv,
                y_send, y_recv, x_send, x_recv, z_send, z_recv, o_sem):
    zyx = place()
    z, y, x = zyx
    dp = lax.axis_index("dp")

    def remote(src, dst, ss, rs_, dev):
        return pltpu.make_async_remote_copy(
            src_ref=src, dst_ref=dst, send_sem=ss, recv_sem=rs_, device_id=dev, device_id_type=MESH)

    loads = [pltpu.make_async_copy(pair_ref, pr.at[0], l_sem.at[0]),
             pltpu.make_async_copy(all_ref.at[0], gq.at[0], l_sem.at[1]),
             pltpu.make_async_copy(others_ref.at[2], gq.at[1], l_sem.at[2]),
             pltpu.make_async_copy(others_ref.at[0], gq.at[2], l_sem.at[3]),
             pltpu.make_async_copy(others_ref.at[1], gq.at[3], l_sem.at[4])]
    for h in range(2):
        at = pl.multiple_of(h * 4096 + (z, y)[h] * 1024, 1024)
        loads.append(pltpu.make_async_copy(w_ref.at[pl.ds(at, 1024)], wv.at[h, 0], l_sem.at[5 + h * 4]))
        for k in (1, 2, 3):
            loads.append(pltpu.make_async_copy(wz_ref.at[h, k], wv.at[h, k], l_sem.at[5 + h * 4 + k]))
    for c in loads:
        c.start()
    hello_all(zyx)
    all_said_hello()
    sends = []

    def go(c):
        c.start()
        sends.append(c)
        return c

    to2 = go(remote(pair_ref, pr.at[2], p_send.at[0], p_recv.at[0], {"dp": dp ^ 2}))
    to1 = go(remote(pair_ref, pr.at[1], p_send.at[1], p_recv.at[1], {"dp": dp ^ 1}))
    def peer(h, t):
        return {"section": t} if h == 0 else {"tensor": t * 2 + x}

    def part(ref, h, e):
        return ref.at[pl.ds(2 * e, 2)] if h == 0 else ref.at[:, pl.ds(2 * e, 2)]

    at = (z, y)
    pz = (pza, pzb)
    for e in range(2):
        for d in (1, 3, 2):
            for h in range(2):
                go(remote(part(pair_ref, h, e), pz[h].at[3 - d, e], s_send.at[h, d - 1, e], s_recv.at[h, 3 - d, e],
                          peer(h, (at[h] + d) % 4)))
    to2.wait_recv()
    to3 = go(remote(pr.at[2], pr.at[3], f_send, f_recv, {"dp": dp ^ 1}))
    to1.wait_recv()
    for c in loads[:5]:
        c.wait()
    to3.wait_recv()

    def wrows(d, j):
        return wg_ref.at[pl.ds(pl.multiple_of(d * 2048 + j * 512, 512), 512)]

    g2, g1, outs = [], [], []

    def wgrad(j):
        cols = pl.ds(j * 512, 512)
        acc = dg(pr[0].reshape(512, 256), gq[0, :, cols], 0, 0)
        for s in (1, 2, 3):
            acc = acc + dg(pr[s].reshape(512, 256), gq[s, :, cols], 0, 0)
        wq[cols] = acc.T.astype(BF).reshape(512, 2, 128)
        g2.append(go(remote(wq.at[cols], wrows(dp, j), g_send.at[0, j], g_recv.at[0, j], {"dp": dp ^ 2})))
        g1.append(go(remote(wq.at[cols], wrows(dp, j), g_send.at[1, j], g_recv.at[1, j], {"dp": dp ^ 1})))
        outs.append(pltpu.make_async_copy(wq.at[cols], wrows(dp, j), o_sem.at[2 + j]))
        outs[-1].start()

    g3 = []

    def pass_on(j):
        g2[j].wait_recv()
        g3.append(go(remote(wrows(dp ^ 2, j), wrows(dp ^ 2, j), h_send.at[j], h_recv.at[j], {"dp": dp ^ 1})))

    for c in loads[5:]:
        c.wait()
    for e in range(2):
        wgrad(2 * e)
        wgrad(2 * e + 1)
        for h in range(2):
            for k in range(3):
                pltpu.make_async_copy(pz[h].at[k, e], pz[h].at[k, e], s_recv.at[h, k, e]).wait()

            def tile_part(j, _, h=h, e=e):
                cols = pl.ds(pl.multiple_of(j * 512, 512), 512)
                rows = part(pr.at[0], h, e)[...].reshape(256, 256)
                acc = dg(rows, wv[h, 0, cols].reshape(512, 256), 1, 1)
                for k in range(3):
                    acc = acc + dg(pz[h][k, e].reshape(256, 256), wv[h, k + 1, cols].reshape(512, 256), 1, 1)
                t = acc.astype(BF)
                for a in range(2 if h == 0 else 4):
                    for b in range(4 if h == 0 else 2):
                        n = (a * 4 + b) if h == 0 else (a * 2 + b)
                        block = t[n * 32:(n + 1) * 32].reshape(2, 16, 512)
                        if h == 0:
                            tp[h, e, b, :, a, :, cols] = block
                        else:
                            tp[h, e, a, :, b, :, cols] = block
                return 0

            lax.fori_loop(0, 2, tile_part, 0)
            for d in (1, 3, 2):
                t = (at[1 - h] + d) % 4
                go(remote(tp.at[h, e, t], rs.at[h, e, 3 - d], y_send.at[h, e, d - 1], y_recv.at[h, e, 3 - d],
                          peer(1 - h, t)))

    for e in range(2):
        for h in range(2):
            for s in range(3):
                pltpu.make_async_copy(rs.at[h, e, s], rs.at[h, e, s], y_recv.at[h, e, s]).wait()
            for f in range(2):
                tot = tp[h, e, at[1 - h], f].astype(F32)
                for s in range(3):
                    tot = tot + rs[h, e, s, f].astype(F32)
                own[h, e, f] = tot
            xs[h, e] = own[h, e, 1 - x].astype(BF)
            go(remote(xs.at[h, e], xr.at[h, e], x_send.at[h, e], x_recv.at[h, e], {"tensor": y * 2 + (1 - x)}))
        pass_on(e)

    for h in range(2):
        for e in range(2):
            pltpu.make_async_copy(xr.at[h, e], xr.at[h, e], x_recv.at[h, e]).wait()
            zs[h, pl.ds(2 * e, 2)] = (own[h, e, x] + xr[h, e].astype(F32)).astype(BF)
        cols = pl.ds(pl.multiple_of(h * 4096 + at[h] * 1024, 1024), 1024)
        for d in (1, 3, 2):
            t = (at[h] + d) % 4
            go(remote(zs.at[h, t], tg_ref.at[:, cols], z_send.at[h, d - 1], z_recv.at[h, 3 - d], peer(h, t)))
        c = pltpu.make_async_copy(zs.at[h, at[h]], tg_ref.at[:, cols], o_sem.at[h])
        c.start()
        outs.append(c)

    pass_on(2)
    pass_on(3)
    for j in range(4):
        g1[j].wait_recv()
        g3[j].wait_recv()
    for h in range(2):
        for d in (1, 2, 3):
            s = (at[h] + d) % 4
            v = tg_ref.at[:, pl.ds(pl.multiple_of(h * 4096 + s * 1024, 1024), 1024)]
            pltpu.make_async_copy(v, v, z_recv.at[h, d - 1]).wait()
    for c in outs:
        c.wait()
    for c in sends:
        c.wait_send()


def tail(pair, others, every_tile, wz, weight):
    hbm = pl.BlockSpec(memory_space=pl.ANY)
    dma = pltpu.SemaphoreType.DMA
    return pl.pallas_call(
        tail_kernel,
        in_specs=[pl.BlockSpec(memory_space=pltpu.HBM)] * 5,
        out_specs=[hbm] * 2,
        out_shape=[jax.ShapeDtypeStruct((16, 8192), BF), jax.ShapeDtypeStruct((8192, 2, 128), BF)],
        scratch_shapes=[
            pltpu.VMEM((3, 2, 2, 4, 32, 256), BF), pltpu.VMEM((3, 2, 4, 2, 32, 256), BF), pltpu.VMEM((4, 4, 4, 32, 256), BF), pltpu.VMEM((4, 512, 2048), BF),
            pltpu.VMEM((2, 4, 1024, 2, 128), BF), pltpu.VMEM((2048, 2, 128), BF),
            pltpu.VMEM((2, 2, 4, 2, 2, 16, 1024), BF), pltpu.VMEM((2, 2, 3, 2, 2, 16, 1024), BF),
            pltpu.VMEM((2, 2, 2, 2, 16, 1024), F32), pltpu.VMEM((2, 2, 2, 16, 1024), BF),
            pltpu.VMEM((2, 2, 2, 16, 1024), BF), pltpu.VMEM((2, 4, 16, 1024), BF),
            dma((13,)), dma((2,)), dma((2,)), dma((2, 3, 2)), dma((2, 3, 2)), dma, dma, dma((2, 4)), dma((2, 4)), dma((4,)), dma((4,)),
            dma((2, 2, 3)), dma((2, 2, 3)), dma((2, 2)), dma((2, 2)), dma((2, 3)), dma((2, 3)), dma((6,))],
        compiler_params=pltpu.CompilerParams(
            vmem_limit_bytes=50 * 2**20, collective_id=2, has_side_effects=True),
    )(pair, others, every_tile, wz, weight)


def local(queries, grad_out, tiles, key_value_matrix, gate, tile_count):
    packed = key_value_matrix.reshape(8192, 2, 128)
    kv, quarters = gather_and_project(tiles, packed)
    query_grad, pair, others, wz = attention(
        queries[0, 0], grad_out[0, 0], kv, tile_count, jnp.tanh(gate), tiles, quarters, packed
    )
    tile_grad, weight_gradient = tail(pair.reshape(4, 4, 32, 256), others, quarters, wz, packed)
    return (query_grad[None, None], tile_grad[None], weight_gradient.reshape(1, 8192, 1, 2, 128))


def solution(mesh):
    return jax.shard_map(
        local,
        mesh=mesh,
        in_specs=(
            P("section", "dp", None, "tensor"),
            P("section", "dp", None, "tensor"),
            P("dp", ("section", "tensor"), None),
            P("section", None, "tensor", None, None),
            P("section"),
            P("dp"),
        ),
        out_specs=(
            P("section", "dp", None, "tensor"),
            P("dp", ("section", "tensor"), None),
            P("section", None, "tensor", None, None),
        ),
        check_vma=False,
    )
```

```python
import functools
import heapq

import jax
import jax.numpy as jnp
from jax import lax
from jax.experimental import pallas as pl
from jax.experimental.pallas import tpu as pltpu
from jax.sharding import PartitionSpec as P

F32, BF = jnp.float32, jnp.bfloat16
SC = 128 ** -0.5
LOG2E = 1.4426950408889634


def dg(a, b, ca, cb):
    return lax.dot_general(a, b, (((ca,), (cb,)), ((), ())), preferred_element_type=F32)

MESH = pl.DeviceIdType.MESH
SIZES = {"z": 4, "y": 4, "x": 2}
AX = "zyx"

def gather_plan(parts, latency=0.3):
    def dirs(a):
        return (1,) if SIZES[a] == 2 else (1, -1)
    def shift(u, a, s):
        u = list(u); n = AX.index(a); u[n] = (u[n] - s) % SIZES[a]
        return tuple(u)
    def sends_of(p, u, via):
        order, _, flip = parts[p]
        out = []
        if via is not None:
            a, s = via
            k = order.index(a)
            if SIZES[a] == 4 and u[AX.index(a)] in (1, 3):
                d = -1 if u[AX.index(a)] == 1 else 1
                par = (sum(u[AX.index(b)] for b in order[:k]) + flip) % 2
                if (d == 1) == (par == 0):
                    out.append((p, u, a, d))
            rest = order[k + 1:]
        else:
            rest = order
        for a in rest:
            for d in dirs(a):
                out.append((p, u, a, d))
        return out
    free = {}
    heap = []
    cnt = 0
    def push(t, sends):
        nonlocal cnt
        for (p, u, a, d) in sends:
            t0 = max(t, free.get((a, d), 0.0))
            t1 = t0 + parts[p][1]
            free[(a, d)] = t1
            cnt += 1
            heapq.heappush(heap, (t1 + latency, cnt, p, shift(u, a, d), (a, d)))
    init = [s for p in range(len(parts)) for s in sends_of(p, (0, 0, 0), None)]
    push(0.0, init)
    events, last = [], 0.0
    while heap:
        t, _, p, u, via = heapq.heappop(heap)
        s = sends_of(p, u, via)
        events.append((t, p, u, s))
        push(t, s)
        last = t
    for p in range(len(parts)):
        got = sorted(u for _, q, u, _ in events if q == p)
        full = 1
        for a in parts[p][0]:
            full *= SIZES[a]
        assert len(got) == len(set(got)) == full - 1
    return init, events, last, dict(free)

def place():
    z = lax.axis_index("section"); t = lax.axis_index("tensor")
    return z, t // 2, t % 2

def neighbour(zyx, a, d):
    z, y, x = zyx
    if a == "z":
        return {"section": (z + d) % 4}
    if a == "y":
        return {"tensor": ((y + d) % 4) * 2 + x}
    return {"tensor": y * 2 + (1 - x)}

def uidx(u):
    return u[0] * 8 + u[1] * 2 + u[2]

def row_of(zyx, u):
    z, y, x = zyx
    return ((z + u[0]) % 4) * 8 + ((y + u[1]) % 4) * 2 + (x + u[2]) % 2

def greet(zyx):
    bar = pltpu.get_barrier_semaphore()
    ns = [("x", 1), ("y", 1), ("y", -1), ("z", 1), ("z", -1)]
    for a, d in ns:
        pl.semaphore_signal(bar, inc=1, device_id=neighbour(zyx, a, d), device_id_type=MESH)
    pl.semaphore_wait(bar, len(ns))

PARTS = {4: [("xyz", 0.6875, 0), ("xzy", 0.6875, 0), ("yzx", 0.3125, 0), ("zyx", 0.3125, 1)]}
COLS = {4: [(0, 2816), (2816, 2816), (5632, 1280), (6912, 1280)]}

def ag_kernel(np_, tiles_ref, w_ref, kv_ref, out_ref, buf, raw, wide, acc, send_sem, recv_sem, loc_sem):
    zyx = place()
    dp = lax.axis_index("dp")
    init, events, _, _ = gather_plan(PARTS[np_], latency=0.7)
    cols = COLS[np_]
    mine = row_of(zyx, (0, 0, 0))
    loc = pltpu.make_async_copy(tiles_ref.at[0], buf.at[pl.ds(pl.multiple_of(mine * 16, 16), 16)], loc_sem.at[0])
    loc.start()
    load_w = pltpu.make_async_copy(w_ref, raw, loc_sem.at[1])
    load_w.start()
    greet(zyx)
    started = []

    def view(ref, p, u):
        return ref.at[pl.ds(pl.multiple_of(row_of(zyx, u) * 16, 16), 16), pl.ds(*cols[p])]

    def start(p, u, a, d):
        n = AX.index(a)
        v = list(u)
        v[n] = (v[n] - d) % SIZES[a]
        src = tiles_ref.at[0, :, pl.ds(*cols[p])] if u == (0, 0, 0) else view(buf, p, u)
        c = pltpu.make_async_remote_copy(
            src_ref=src, dst_ref=view(buf, p, u),
            send_sem=send_sem.at[len(started)], recv_sem=recv_sem.at[p * 32 + uidx(v)],
            device_id=neighbour(zyx, a, d), device_id_type=MESH)
        c.start()
        started.append(c)

    def wait(p, u):
        v = view(buf, p, u)
        pltpu.make_async_copy(v, v, recv_sem.at[p * 32 + uidx(u)]).wait()

    for s in init:
        start(*s)
    done = 0
    for n, (_, p, u, sends) in enumerate(events):
        wait(p, u)
        for s in sends:
            start(*s)
        if n % 12 == 5 and done < 8:
            if done == 0:
                load_w.wait()
            rows = pl.ds(done * 1024, 1024)
            wide[rows] = raw[rows].reshape(1024, 256)
            done += 1
    assert done == 8
    loc.wait()
    outs = []
    for k in range(2):
        c = pltpu.make_async_copy(
            buf.at[:, pl.ds(pl.multiple_of((dp ^ k) * 2048, 2048), 2048)], out_ref.at[k], loc_sem.at[2 + k])
        c.start()
        outs.append(c)
    acc[...] = jnp.zeros_like(acc)

    def project(j, _):
        at = pl.ds(pl.multiple_of(j * 1024, 1024), 1024)
        acc[...] += dg(buf[:, at], wide[at], 1, 0)
        return 0

    lax.fori_loop(0, 8, project, 0)
    kv_ref[...] = acc[...].astype(BF)
    for c in started:
        c.wait_send()
    for c in outs:
        c.wait()


def nsends(np_):
    init, events, _, _ = gather_plan(PARTS[np_], latency=0.7)
    return len(init) + sum(len(e[3]) for e in events)


def gather_and_project(tiles, weight, np_=4, cid=0):
    dma = pltpu.SemaphoreType.DMA
    hbm = pl.BlockSpec(memory_space=pl.ANY)
    return pl.pallas_call(
        functools.partial(ag_kernel, np_),
        in_specs=[hbm, hbm],
        out_specs=[pl.BlockSpec(memory_space=pltpu.VMEM), hbm],
        out_shape=[jax.ShapeDtypeStruct((512, 256), BF), jax.ShapeDtypeStruct((2, 512, 2048), BF)],
        scratch_shapes=[
            pltpu.VMEM((512, 8192), BF), pltpu.VMEM((8192, 2, 128), BF), pltpu.VMEM((8192, 256), BF),
            pltpu.VMEM((512, 256), F32), dma((nsends(np_),)), dma((np_ * 32,)), dma((4,))],
        compiler_params=pltpu.CompilerParams(
            vmem_limit_bytes=60 * 2**20, collective_id=cid, has_side_effects=True),
    )(tiles, weight)


def attention_rows(lay, sub, f, cnt, q_ref, g_ref, kv_ref, dq_ref, ka, va, opt=""):
    k = kv_ref[:, :128]; v = kv_ref[:, 128:]
    J = k.shape[0]; R = q_ref.shape[0]; H = J // 2
    ax = 0 if lay == "T" else 1
    valid = lax.broadcasted_iota(jnp.int32, (H, 1) if ax == 0 else (1, H), ax) + H < cnt
    items = [(h, r) for r in range(R // sub) for h in range(8)]
    def first(it):
        h, r = it
        rs = pl.ds(r * sub, sub); c = pl.ds(h * 128, 128)
        q = q_ref[rs, c]; g = (f * g_ref[rs, c].astype(F32)).astype(BF)
        if lay == "T": return q, g, dg(k, q, 1, 1), dg(v, g, 1, 1)
        return q, g, dg(q, k, 1, 1), dg(g, v, 1, 1)
    def mid(q, g, s, dp):
        if ax == 0: s = jnp.concatenate([s[:H], jnp.where(valid, s[H:], -jnp.inf)], axis=0)
        else: s = jnp.concatenate([s[:, :H], jnp.where(valid, s[:, H:], -jnp.inf)], axis=1)
        m = jnp.max(s, axis=ax, keepdims=True)
        e = jnp.exp2((s - m) * (SC * LOG2E))
        inv = 1.0 / jnp.sum(e, axis=ax, keepdims=True)
        delta = jnp.sum(e * dp, axis=ax, keepdims=True) * inv
        ph = (e * inv).astype(BF)
        ds = ((e * (inv * SC)) * (dp - delta)).astype(BF)
        return ds, ph
    def last(it, q, g, ds, ph):
        h, r = it
        o = (pl.ds(r * sub, sub), pl.ds(h * 128, 128))
        if lay == "T":
            dq_ref[o] = dg(k, ds, 0, 0).T.astype(BF)
            ka[...] += dg(ds, q, 1, 0); va[...] += dg(ph, g, 1, 0)
        else:
            dq_ref[o] = dg(ds, k, 1, 0).astype(BF)
            ka[...] += dg(q, ds, 0, 0); va[...] += dg(g, ph, 0, 0)
    nxt = first(items[0]); prev = None
    for n, it in enumerate(items):
        cur = nxt
        if n + 1 < len(items): nxt = first(items[n + 1])
        if prev is not None: last(*prev)
        b = mid(*cur)
        prev = (it, cur[0], cur[1], *b)
    last(*prev)


def background_plan(steps, unit_us=4.0, start_us=12.0, step_us=3.5):
    parts = [("zy", 1.0, 0), ("yz", 1.0, 1)]
    init, events, _, _ = gather_plan(parts, latency=0.7)
    per_step = [[] for _ in range(steps)]
    for t, p, u, sends in events:
        n = int((start_us + t * unit_us) / step_us) + 1
        per_step[min(n, steps - 1)].append((p, u, sends))
    return init, per_step


def count_sends(init, per_step):
    return len(init) + sum(len(e[2]) for b in per_step for e in b)


def hello_all(zyx):
    z, y, x = zyx
    dp = lax.axis_index("dp")
    peers = [{"section": (z + d) % 4} for d in (1, 2, 3)]
    peers += [{"tensor": ((y + d) % 4) * 2 + x} for d in (1, 2, 3)]
    peers += [{"tensor": y * 2 + (1 - x)}]
    peers += [{"dp": dp ^ k} for k in (1, 2, 3)]
    for d in peers:
        pl.semaphore_signal(pltpu.get_barrier_semaphore(), inc=1, device_id=d, device_id_type=MESH)


def all_said_hello():
    pl.semaphore_wait(pltpu.get_barrier_semaphore(), 10)


def attention_kernel(steps, cnt_ref, fac_ref, q_ref, g_ref, kv_ref, tiles_ref, all_ref, w_ref,
                     dq_ref, pair_ref, others_ref, wz_ref, ka, va,
                     send_sem, recv_sem, swap_send, swap_recv, e_send, e_recv, w_send, w_recv, c_send, c_recv, x_send, x_recv):
    i = pl.program_id(0)
    zyx = place()
    z, y, x = zyx
    dp = lax.axis_index("dp")
    core = dp % 2
    init, per_step = background_plan(steps)
    started = []

    def rows(u):
        return pl.ds(pl.multiple_of(row_of(zyx, u) * 16, 16), 16)

    def pair_rows(u):
        at = ((z + u[0]) % 4) * 8 + ((y + u[1]) % 4) * 2
        return pl.ds(pl.multiple_of(at * 16, 32), 32)

    def quarter(d):
        return pl.ds(pl.multiple_of(d * 2048, 2048), 2048)

    def part_copy(p, u, a, d, at=None):
        if at is None:
            at = len(started)
            started.append((p, u, a, d, at))
        n = AX.index(a)
        v = list(u)
        v[n] = (v[n] - d) % SIZES[a]
        c = pltpu.make_async_remote_copy(
            src_ref=others_ref.at[p, pair_rows(u)], dst_ref=others_ref.at[p, pair_rows(u)],
            send_sem=send_sem.at[at], recv_sem=recv_sem.at[p * 32 + uidx(v)],
            device_id=neighbour(zyx, a, d), device_id_type=MESH)
        return c

    def landed(ref, sem):
        pltpu.make_async_copy(ref, ref, sem).wait()

    def swap(p):
        return pltpu.make_async_remote_copy(
            src_ref=tiles_ref.at[0, :, quarter(dp ^ (2 + p))], dst_ref=others_ref.at[p, rows((0, 0, 0))],
            send_sem=swap_send.at[p], recv_sem=swap_recv.at[p], device_id={"dp": dp ^ (2 + p)}, device_id_type=MESH)

    def across(p, far=0):
        u = others_ref.at[p, rows((0, 0, far))]
        return pltpu.make_async_remote_copy(
            src_ref=u, dst_ref=u, send_sem=e_send.at[p], recv_sem=e_recv.at[p],
            device_id=neighbour(zyx, "x", 1), device_id_type=MESH)

    def w_copy(h, d):
        t = ((z, y)[h] + d) % 4
        dev = {"section": t} if h == 0 else {"tensor": t * 2 + x}
        return pltpu.make_async_remote_copy(
            src_ref=w_ref.at[pl.ds(pl.multiple_of(h * 4096 + t * 1024 + core * 512, 512), 512)],
            dst_ref=wz_ref.at[h, 4 - d, pl.ds(pl.multiple_of(core * 512, 512), 512)],
            send_sem=w_send.at[h, d - 1], recv_sem=w_recv.at[h, 3 - d], device_id=dev, device_id_type=MESH)

    def half(h, k, c):
        return wz_ref.at[h, k, pl.ds(pl.multiple_of(c * 512, 512), 512)]

    def c_copy(h, k):
        return pltpu.make_async_remote_copy(
            src_ref=half(h, k, core), dst_ref=half(h, k, core), send_sem=c_send.at[h, k - 1],
            recv_sem=c_recv.at[h, k - 1], device_id={"dp": dp ^ 1}, device_id_type=MESH)

    def x_copy():
        return pltpu.make_async_remote_copy(
            src_ref=all_ref.at[1], dst_ref=others_ref.at[2],
            send_sem=x_send, recv_sem=x_recv, device_id={"dp": dp ^ 1}, device_id_type=MESH)

    @pl.when(i == 0)
    def _():
        ka[...] = jnp.zeros_like(ka)
        va[...] = jnp.zeros_like(va)
        hello_all(zyx)

    for n in range(1, steps):
        def batch(n=n):
            if n == 1:
                all_said_hello()
                for p in (0, 1):
                    swap(p).start()
                for d in (1, 3):
                    for h in (0, 1):
                        w_copy(h, d).start()
                x_copy().start()
            if n == 2:
                for p in (0, 1):
                    landed(others_ref.at[p, rows((0, 0, 0))], swap_recv.at[p])
                    across(p).start()
            if n == 3:
                for p in (0, 1):
                    landed(others_ref.at[p, rows((0, 0, 1))], e_recv.at[p])
                for s in init:
                    part_copy(*s).start()
            for p, u, sends in per_step[n]:
                landed(others_ref.at[p, pair_rows(u)], recv_sem.at[p * 32 + uidx(u)])
                for s in sends:
                    part_copy(*s).start()
            if n == 9:
                for h in (0, 1):
                    w_copy(h, 2).start()
            if n == steps - 1:
                for k in (1, 3, 2):
                    for h in (0, 1):
                        landed(half(h, k, core), w_recv.at[h, k - 1])
                        c_copy(h, k).start()
        assert n >= 4 or not per_step[n]
        if n in (1, 2, 3, 9, steps - 1) or per_step[n]:
            pl.when(i == n)(batch)

    attention_rows("L", q_ref.shape[0], fac_ref[0], cnt_ref[0], q_ref, g_ref, kv_ref, dq_ref, ka, va)

    @pl.when(i == steps - 1)
    def _():
        pair_ref[:, :128] = ka[...].T.astype(BF)
        pair_ref[:, 128:] = va[...].T.astype(BF)
        for s in started:
            part_copy(*s).wait_send()
        for p in (0, 1):
            swap(p).wait_send()
        for p in (0, 1):
            across(p).wait_send()
        for h in (0, 1):
            for d in (1, 2, 3):
                w_copy(h, d).wait_send()
            for k in (1, 2, 3):
                c_copy(h, k).wait_send()
                landed(half(h, k, 1 - core), c_recv.at[h, k - 1])
        x_copy().wait()


def attention(q, g, kv, cnt, fac, tiles, every_tile, weight, R=256):
    n = q.shape[0]
    steps = n // R
    hbm = pl.BlockSpec(memory_space=pl.ANY)
    dma = pltpu.SemaphoreType.DMA
    return pl.pallas_call(
        functools.partial(attention_kernel, steps),
        grid=(steps,),
        in_specs=[pl.BlockSpec(memory_space=pltpu.SMEM)] * 2 + [
            pl.BlockSpec((R, 1024), lambda i: (i, 0)),
            pl.BlockSpec((R, 1024), lambda i: (i, 0)),
            pl.BlockSpec((512, 256), lambda i: (0, 0)), hbm, hbm, hbm],
        out_specs=[pl.BlockSpec((R, 1024), lambda i: (i, 0)), pl.BlockSpec((512, 256), lambda i: (0, 0)), hbm, hbm],
        out_shape=[jax.ShapeDtypeStruct((n, 1024), BF), jax.ShapeDtypeStruct((512, 256), BF),
                   jax.ShapeDtypeStruct((3, 512, 2048), BF), jax.ShapeDtypeStruct((2, 4, 1024, 2, 128), BF)],
        scratch_shapes=[pltpu.VMEM((128, 512), F32)] * 2 + [
            dma((count_sends(*background_plan(steps)),)), dma((64,)), dma((2,)), dma((2,)), dma((2,)), dma((2,)),
            dma((2, 3)), dma((2, 3)), dma((2, 3)), dma((2, 3)), dma, dma],
        compiler_params=pltpu.CompilerParams(
            vmem_limit_bytes=60 * 2**20, dimension_semantics=("arbitrary",), collective_id=1, has_side_effects=True),
    )(cnt, fac, q, g, kv, tiles, every_tile, weight)


def tail_kernel(pair_ref, others_ref, all_ref, wz_ref, w_ref, tg_ref, wg_ref,
                pza, pzb, pr, gq, wv, wq, tp, rs, own, xs, xr, zs,
                l_sem, p_send, p_recv, s_send, s_recv, f_send, f_recv, g_send, g_recv, h_send, h_recv,
                y_send, y_recv, x_send, x_recv, z_send, z_recv, o_sem):
    zyx = place()
    z, y, x = zyx
    dp = lax.axis_index("dp")

    def remote(src, dst, ss, rs_, dev):
        return pltpu.make_async_remote_copy(
            src_ref=src, dst_ref=dst, send_sem=ss, recv_sem=rs_, device_id=dev, device_id_type=MESH)

    loads = [pltpu.make_async_copy(pair_ref, pr.at[0], l_sem.at[0]),
             pltpu.make_async_copy(all_ref.at[0], gq.at[0], l_sem.at[1]),
             pltpu.make_async_copy(others_ref.at[2], gq.at[1], l_sem.at[2]),
             pltpu.make_async_copy(others_ref.at[0], gq.at[2], l_sem.at[3]),
             pltpu.make_async_copy(others_ref.at[1], gq.at[3], l_sem.at[4])]
    for h in range(2):
        at = pl.multiple_of(h * 4096 + (z, y)[h] * 1024, 1024)
        loads.append(pltpu.make_async_copy(w_ref.at[pl.ds(at, 1024)], wv.at[h, 0], l_sem.at[5 + h * 4]))
        for k in (1, 2, 3):
            loads.append(pltpu.make_async_copy(wz_ref.at[h, k], wv.at[h, k], l_sem.at[5 + h * 4 + k]))
    for c in loads:
        c.start()
    hello_all(zyx)
    all_said_hello()
    sends = []

    def go(c):
        c.start()
        sends.append(c)
        return c

    to2 = go(remote(pair_ref, pr.at[2], p_send.at[0], p_recv.at[0], {"dp": dp ^ 2}))
    to1 = go(remote(pair_ref, pr.at[1], p_send.at[1], p_recv.at[1], {"dp": dp ^ 1}))
    def peer(h, t):
        return {"section": t} if h == 0 else {"tensor": t * 2 + x}

    def part(ref, h, e):
        return ref.at[pl.ds(2 * e, 2)] if h == 0 else ref.at[:, pl.ds(2 * e, 2)]

    at = (z, y)
    pz = (pza, pzb)
    for e in range(2):
        for d in (1, 3, 2):
            for h in range(2):
                go(remote(part(pair_ref, h, e), pz[h].at[3 - d, e], s_send.at[h, d - 1, e], s_recv.at[h, 3 - d, e],
                          peer(h, (at[h] + d) % 4)))
    to2.wait_recv()
    to3 = go(remote(pr.at[2], pr.at[3], f_send, f_recv, {"dp": dp ^ 1}))
    to1.wait_recv()
    for c in loads[:5]:
        c.wait()
    to3.wait_recv()

    def wrows(d, j):
        return wg_ref.at[pl.ds(pl.multiple_of(d * 2048 + j * 512, 512), 512)]

    g2, g1, outs = [], [], []

    def wgrad(j):
        cols = pl.ds(j * 512, 512)
        acc = dg(pr[0].reshape(512, 256), gq[0, :, cols], 0, 0)
        for s in (1, 2, 3):
            acc = acc + dg(pr[s].reshape(512, 256), gq[s, :, cols], 0, 0)
        wq[cols] = acc.T.astype(BF).reshape(512, 2, 128)
        g2.append(go(remote(wq.at[cols], wrows(dp, j), g_send.at[0, j], g_recv.at[0, j], {"dp": dp ^ 2})))
        g1.append(go(remote(wq.at[cols], wrows(dp, j), g_send.at[1, j], g_recv.at[1, j], {"dp": dp ^ 1})))
        outs.append(pltpu.make_async_copy(wq.at[cols], wrows(dp, j), o_sem.at[2 + j]))
        outs[-1].start()

    g3 = []

    def pass_on(j):
        g2[j].wait_recv()
        g3.append(go(remote(wrows(dp ^ 2, j), wrows(dp ^ 2, j), h_send.at[j], h_recv.at[j], {"dp": dp ^ 1})))

    for c in loads[5:]:
        c.wait()
    for e in range(2):
        wgrad(2 * e)
        wgrad(2 * e + 1)
        for h in range(2):
            for k in range(3):
                pltpu.make_async_copy(pz[h].at[k, e], pz[h].at[k, e], s_recv.at[h, k, e]).wait()

            def tile_part(j, _, h=h, e=e):
                cols = pl.ds(pl.multiple_of(j * 512, 512), 512)
                rows = part(pr.at[0], h, e)[...].reshape(256, 256)
                acc = dg(rows, wv[h, 0, cols].reshape(512, 256), 1, 1)
                for k in range(3):
                    acc = acc + dg(pz[h][k, e].reshape(256, 256), wv[h, k + 1, cols].reshape(512, 256), 1, 1)
                t = acc.astype(BF)
                for a in range(2 if h == 0 else 4):
                    for b in range(4 if h == 0 else 2):
                        n = (a * 4 + b) if h == 0 else (a * 2 + b)
                        block = t[n * 32:(n + 1) * 32].reshape(2, 16, 512)
                        if h == 0:
                            tp[h, e, b, :, a, :, cols] = block
                        else:
                            tp[h, e, a, :, b, :, cols] = block
                return 0

            lax.fori_loop(0, 2, tile_part, 0)
            for d in (1, 3, 2):
                t = (at[1 - h] + d) % 4
                go(remote(tp.at[h, e, t], rs.at[h, e, 3 - d], y_send.at[h, e, d - 1], y_recv.at[h, e, 3 - d],
                          peer(1 - h, t)))

    for e in range(2):
        for h in range(2):
            for s in range(3):
                pltpu.make_async_copy(rs.at[h, e, s], rs.at[h, e, s], y_recv.at[h, e, s]).wait()
            for f in range(2):
                tot = tp[h, e, at[1 - h], f].astype(F32)
                for s in range(3):
                    tot = tot + rs[h, e, s, f].astype(F32)
                own[h, e, f] = tot
            xs[h, e] = own[h, e, 1 - x].astype(BF)
            go(remote(xs.at[h, e], xr.at[h, e], x_send.at[h, e], x_recv.at[h, e], {"tensor": y * 2 + (1 - x)}))
        pass_on(e)

    for h in range(2):
        for e in range(2):
            pltpu.make_async_copy(xr.at[h, e], xr.at[h, e], x_recv.at[h, e]).wait()
            zs[h, pl.ds(2 * e, 2)] = (own[h, e, x] + xr[h, e].astype(F32)).astype(BF)
        cols = pl.ds(pl.multiple_of(h * 4096 + at[h] * 1024, 1024), 1024)
        for d in (1, 3, 2):
            t = (at[h] + d) % 4
            go(remote(zs.at[h, t], tg_ref.at[:, cols], z_send.at[h, d - 1], z_recv.at[h, 3 - d], peer(h, t)))
        c = pltpu.make_async_copy(zs.at[h, at[h]], tg_ref.at[:, cols], o_sem.at[h])
        c.start()
        outs.append(c)

    pass_on(2)
    pass_on(3)
    for j in range(4):
        g1[j].wait_recv()
        g3[j].wait_recv()
    for h in range(2):
        for d in (1, 2, 3):
            s = (at[h] + d) % 4
            v = tg_ref.at[:, pl.ds(pl.multiple_of(h * 4096 + s * 1024, 1024), 1024)]
            pltpu.make_async_copy(v, v, z_recv.at[h, d - 1]).wait()
    for c in outs:
        c.wait()
    for c in sends:
        c.wait_send()


def tail(pair, others, every_tile, wz, weight):
    hbm = pl.BlockSpec(memory_space=pl.ANY)
    dma = pltpu.SemaphoreType.DMA
    return pl.pallas_call(
        tail_kernel,
        in_specs=[pl.BlockSpec(memory_space=pltpu.HBM)] * 5,
        out_specs=[hbm] * 2,
        out_shape=[jax.ShapeDtypeStruct((16, 8192), BF), jax.ShapeDtypeStruct((8192, 2, 128), BF)],
        scratch_shapes=[
            pltpu.VMEM((3, 2, 2, 4, 32, 256), BF), pltpu.VMEM((3, 2, 4, 2, 32, 256), BF), pltpu.VMEM((4, 4, 4, 32, 256), BF), pltpu.VMEM((4, 512, 2048), BF),
            pltpu.VMEM((2, 4, 1024, 2, 128), BF), pltpu.VMEM((2048, 2, 128), BF),
            pltpu.VMEM((2, 2, 4, 2, 2, 16, 1024), BF), pltpu.VMEM((2, 2, 3, 2, 2, 16, 1024), BF),
            pltpu.VMEM((2, 2, 2, 2, 16, 1024), F32), pltpu.VMEM((2, 2, 2, 16, 1024), BF),
            pltpu.VMEM((2, 2, 2, 16, 1024), BF), pltpu.VMEM((2, 4, 16, 1024), BF),
            dma((13,)), dma((2,)), dma((2,)), dma((2, 3, 2)), dma((2, 3, 2)), dma, dma, dma((2, 4)), dma((2, 4)), dma((4,)), dma((4,)),
            dma((2, 2, 3)), dma((2, 2, 3)), dma((2, 2)), dma((2, 2)), dma((2, 3)), dma((2, 3)), dma((6,))],
        compiler_params=pltpu.CompilerParams(
            vmem_limit_bytes=50 * 2**20, collective_id=2, has_side_effects=True),
    )(pair, others, every_tile, wz, weight)


def local(queries, grad_out, tiles, key_value_matrix, gate, tile_count):
    packed = key_value_matrix.reshape(8192, 2, 128)
    kv, quarters = gather_and_project(tiles, packed)
    query_grad, pair, others, wz = attention(
        queries[0, 0], grad_out[0, 0], kv, tile_count, jnp.tanh(gate), tiles, quarters, packed
    )
    tile_grad, weight_gradient = tail(pair.reshape(4, 4, 32, 256), others, quarters, wz, packed)
    return (query_grad[None, None], tile_grad[None], weight_gradient.reshape(1, 8192, 1, 2, 128))


def solution(mesh):
    return jax.shard_map(
        local,
        mesh=mesh,
        in_specs=(
            P("section", "dp", None, "tensor"),
            P("section", "dp", None, "tensor"),
            P("dp", ("section", "tensor"), None),
            P("section", None, "tensor", None, None),
            P("section"),
            P("dp"),
        ),
        out_specs=(
            P("section", "dp", None, "tensor"),
            P("dp", ("section", "tensor"), None),
            P("section", None, "tensor", None, None),
        ),
        check_vma=False,
    )
```

```python
import functools
import heapq

import jax
import jax.numpy as jnp
from jax import lax
from jax.experimental import pallas as pl
from jax.experimental.pallas import tpu as pltpu
from jax.sharding import PartitionSpec as P

F32, BF = jnp.float32, jnp.bfloat16
SC = 128 ** -0.5
LOG2E = 1.4426950408889634


def dg(a, b, ca, cb):
    return lax.dot_general(a, b, (((ca,), (cb,)), ((), ())), preferred_element_type=F32)

MESH = pl.DeviceIdType.MESH
SIZES = {"z": 4, "y": 4, "x": 2}
AX = "zyx"

def gather_plan(parts, latency=0.3):
    def dirs(a):
        return (1,) if SIZES[a] == 2 else (1, -1)
    def shift(u, a, s):
        u = list(u); n = AX.index(a); u[n] = (u[n] - s) % SIZES[a]
        return tuple(u)
    def sends_of(p, u, via):
        order, _, flip = parts[p]
        out = []
        if via is not None:
            a, s = via
            k = order.index(a)
            if SIZES[a] == 4 and u[AX.index(a)] in (1, 3):
                d = -1 if u[AX.index(a)] == 1 else 1
                par = (sum(u[AX.index(b)] for b in order[:k]) + flip) % 2
                if (d == 1) == (par == 0):
                    out.append((p, u, a, d))
            rest = order[k + 1:]
        else:
            rest = order
        for a in rest:
            for d in dirs(a):
                out.append((p, u, a, d))
        return out
    free = {}
    heap = []
    cnt = 0
    def push(t, sends):
        nonlocal cnt
        for (p, u, a, d) in sends:
            t0 = max(t, free.get((a, d), 0.0))
            t1 = t0 + parts[p][1]
            free[(a, d)] = t1
            cnt += 1
            heapq.heappush(heap, (t1 + latency, cnt, p, shift(u, a, d), (a, d)))
    init = [s for p in range(len(parts)) for s in sends_of(p, (0, 0, 0), None)]
    push(0.0, init)
    events, last = [], 0.0
    while heap:
        t, _, p, u, via = heapq.heappop(heap)
        s = sends_of(p, u, via)
        events.append((t, p, u, s))
        push(t, s)
        last = t
    for p in range(len(parts)):
        got = sorted(u for _, q, u, _ in events if q == p)
        full = 1
        for a in parts[p][0]:
            full *= SIZES[a]
        assert len(got) == len(set(got)) == full - 1
    return init, events, last, dict(free)

def place():
    z = lax.axis_index("section"); t = lax.axis_index("tensor")
    return z, t // 2, t % 2

def neighbour(zyx, a, d):
    z, y, x = zyx
    if a == "z":
        return {"section": (z + d) % 4}
    if a == "y":
        return {"tensor": ((y + d) % 4) * 2 + x}
    return {"tensor": y * 2 + (1 - x)}

def uidx(u):
    return u[0] * 8 + u[1] * 2 + u[2]

def row_of(zyx, u):
    z, y, x = zyx
    return ((z + u[0]) % 4) * 8 + ((y + u[1]) % 4) * 2 + (x + u[2]) % 2

def greet(zyx):
    bar = pltpu.get_barrier_semaphore()
    ns = [("x", 1), ("y", 1), ("y", -1), ("z", 1), ("z", -1)]
    for a, d in ns:
        pl.semaphore_signal(bar, inc=1, device_id=neighbour(zyx, a, d), device_id_type=MESH)
    pl.semaphore_wait(bar, len(ns))

PARTS = {4: [("xyz", 0.6875, 0), ("xzy", 0.6875, 0), ("yzx", 0.3125, 0), ("zyx", 0.3125, 1)]}
COLS = {4: [(0, 2816), (2816, 2816), (5632, 1280), (6912, 1280)]}

def ag_kernel(np_, tiles_ref, w_ref, kv_ref, out_ref, buf, raw, wide, acc, send_sem, recv_sem, loc_sem):
    zyx = place()
    dp = lax.axis_index("dp")
    init, events, _, _ = gather_plan(PARTS[np_], latency=1.1)
    cols = COLS[np_]
    mine = row_of(zyx, (0, 0, 0))
    loc = pltpu.make_async_copy(tiles_ref.at[0], buf.at[pl.ds(pl.multiple_of(mine * 16, 16), 16)], loc_sem.at[0])
    loc.start()
    load_w = pltpu.make_async_copy(w_ref, raw, loc_sem.at[1])
    load_w.start()
    greet(zyx)
    started = []

    def view(ref, p, u):
        return ref.at[pl.ds(pl.multiple_of(row_of(zyx, u) * 16, 16), 16), pl.ds(*cols[p])]

    def start(p, u, a, d):
        n = AX.index(a)
        v = list(u)
        v[n] = (v[n] - d) % SIZES[a]
        src = tiles_ref.at[0, :, pl.ds(*cols[p])] if u == (0, 0, 0) else view(buf, p, u)
        c = pltpu.make_async_remote_copy(
            src_ref=src, dst_ref=view(buf, p, u),
            send_sem=send_sem.at[len(started)], recv_sem=recv_sem.at[p * 32 + uidx(v)],
            device_id=neighbour(zyx, a, d), device_id_type=MESH)
        c.start()
        started.append(c)

    def wait(p, u):
        v = view(buf, p, u)
        pltpu.make_async_copy(v, v, recv_sem.at[p * 32 + uidx(u)]).wait()

    for s in init:
        start(*s)
    done = 0
    for n, (_, p, u, sends) in enumerate(events):
        wait(p, u)
        for s in sends:
            start(*s)
        if n % 12 == 5 and done < 8:
            if done == 0:
                load_w.wait()
            rows = pl.ds(done * 1024, 1024)
            wide[rows] = raw[rows].reshape(1024, 256)
            done += 1
    assert done == 8
    loc.wait()
    outs = []
    for k in range(2):
        c = pltpu.make_async_copy(
            buf.at[:, pl.ds(pl.multiple_of((dp ^ k) * 2048, 2048), 2048)], out_ref.at[k], loc_sem.at[2 + k])
        c.start()
        outs.append(c)
    acc[...] = jnp.zeros_like(acc)

    def project(j, _):
        at = pl.ds(pl.multiple_of(j * 1024, 1024), 1024)
        acc[...] += dg(buf[:, at], wide[at], 1, 0)
        return 0

    lax.fori_loop(0, 8, project, 0)
    kv_ref[...] = acc[...].astype(BF)
    for c in started:
        c.wait_send()
    for c in outs:
        c.wait()


def nsends(np_):
    init, events, _, _ = gather_plan(PARTS[np_], latency=1.1)
    return len(init) + sum(len(e[3]) for e in events)


def gather_and_project(tiles, weight, np_=4, cid=0):
    dma = pltpu.SemaphoreType.DMA
    hbm = pl.BlockSpec(memory_space=pl.ANY)
    return pl.pallas_call(
        functools.partial(ag_kernel, np_),
        in_specs=[hbm, hbm],
        out_specs=[pl.BlockSpec(memory_space=pltpu.VMEM), hbm],
        out_shape=[jax.ShapeDtypeStruct((512, 256), BF), jax.ShapeDtypeStruct((2, 512, 2048), BF)],
        scratch_shapes=[
            pltpu.VMEM((512, 8192), BF), pltpu.VMEM((8192, 2, 128), BF), pltpu.VMEM((8192, 256), BF),
            pltpu.VMEM((512, 256), F32), dma((nsends(np_),)), dma((np_ * 32,)), dma((4,))],
        compiler_params=pltpu.CompilerParams(
            vmem_limit_bytes=60 * 2**20, collective_id=cid, has_side_effects=True),
    )(tiles, weight)


def attention_rows(lay, sub, f, cnt, q_ref, g_ref, kv_ref, dq_ref, ka, va, opt=""):
    k = kv_ref[:, :128]; v = kv_ref[:, 128:]
    J = k.shape[0]; R = q_ref.shape[0]; H = J // 2
    ax = 0 if lay == "T" else 1
    valid = lax.broadcasted_iota(jnp.int32, (H, 1) if ax == 0 else (1, H), ax) + H < cnt
    items = [(h, r) for r in range(R // sub) for h in range(8)]
    def first(it):
        h, r = it
        rs = pl.ds(r * sub, sub); c = pl.ds(h * 128, 128)
        q = q_ref[rs, c]; g = (f * g_ref[rs, c].astype(F32)).astype(BF)
        if lay == "T": return q, g, dg(k, q, 1, 1), dg(v, g, 1, 1)
        return q, g, dg(q, k, 1, 1), dg(g, v, 1, 1)
    def mid(q, g, s, dp):
        if ax == 0: s = jnp.concatenate([s[:H], jnp.where(valid, s[H:], -jnp.inf)], axis=0)
        else: s = jnp.concatenate([s[:, :H], jnp.where(valid, s[:, H:], -jnp.inf)], axis=1)
        m = jnp.max(s, axis=ax, keepdims=True)
        e = jnp.exp2((s - m) * (SC * LOG2E))
        inv = 1.0 / jnp.sum(e, axis=ax, keepdims=True)
        delta = jnp.sum(e * dp, axis=ax, keepdims=True) * inv
        ph = (e * inv).astype(BF)
        ds = ((e * (inv * SC)) * (dp - delta)).astype(BF)
        return ds, ph
    def last(it, q, g, ds, ph):
        h, r = it
        o = (pl.ds(r * sub, sub), pl.ds(h * 128, 128))
        if lay == "T":
            dq_ref[o] = dg(k, ds, 0, 0).T.astype(BF)
            ka[...] += dg(ds, q, 1, 0); va[...] += dg(ph, g, 1, 0)
        else:
            dq_ref[o] = dg(ds, k, 1, 0).astype(BF)
            ka[...] += dg(q, ds, 0, 0); va[...] += dg(g, ph, 0, 0)
    nxt = first(items[0]); prev = None
    for n, it in enumerate(items):
        cur = nxt
        if n + 1 < len(items): nxt = first(items[n + 1])
        if prev is not None: last(*prev)
        b = mid(*cur)
        prev = (it, cur[0], cur[1], *b)
    last(*prev)


def background_plan(steps, unit_us=4.0, start_us=12.0, step_us=3.5):
    parts = [("zy", 1.0, 0), ("yz", 1.0, 1)]
    init, events, _, _ = gather_plan(parts, latency=0.7)
    per_step = [[] for _ in range(steps)]
    for t, p, u, sends in events:
        n = int((start_us + t * unit_us) / step_us) + 1
        per_step[min(n, steps - 1)].append((p, u, sends))
    return init, per_step


def count_sends(init, per_step):
    return len(init) + sum(len(e[2]) for b in per_step for e in b)


def hello_all(zyx):
    z, y, x = zyx
    dp = lax.axis_index("dp")
    peers = [{"section": (z + d) % 4} for d in (1, 2, 3)]
    peers += [{"tensor": ((y + d) % 4) * 2 + x} for d in (1, 2, 3)]
    peers += [{"tensor": y * 2 + (1 - x)}]
    peers += [{"dp": dp ^ k} for k in (1, 2, 3)]
    for d in peers:
        pl.semaphore_signal(pltpu.get_barrier_semaphore(), inc=1, device_id=d, device_id_type=MESH)


def all_said_hello():
    pl.semaphore_wait(pltpu.get_barrier_semaphore(), 10)


def attention_kernel(steps, cnt_ref, fac_ref, q_ref, g_ref, kv_ref, tiles_ref, all_ref, w_ref,
                     dq_ref, pair_ref, others_ref, wz_ref, ka, va,
                     send_sem, recv_sem, swap_send, swap_recv, e_send, e_recv, w_send, w_recv, c_send, c_recv, x_send, x_recv):
    i = pl.program_id(0)
    zyx = place()
    z, y, x = zyx
    dp = lax.axis_index("dp")
    core = dp % 2
    init, per_step = background_plan(steps)
    started = []

    def rows(u):
        return pl.ds(pl.multiple_of(row_of(zyx, u) * 16, 16), 16)

    def pair_rows(u):
        at = ((z + u[0]) % 4) * 8 + ((y + u[1]) % 4) * 2
        return pl.ds(pl.multiple_of(at * 16, 32), 32)

    def quarter(d):
        return pl.ds(pl.multiple_of(d * 2048, 2048), 2048)

    def part_copy(p, u, a, d, at=None):
        if at is None:
            at = len(started)
            started.append((p, u, a, d, at))
        n = AX.index(a)
        v = list(u)
        v[n] = (v[n] - d) % SIZES[a]
        c = pltpu.make_async_remote_copy(
            src_ref=others_ref.at[p, pair_rows(u)], dst_ref=others_ref.at[p, pair_rows(u)],
            send_sem=send_sem.at[at], recv_sem=recv_sem.at[p * 32 + uidx(v)],
            device_id=neighbour(zyx, a, d), device_id_type=MESH)
        return c

    def landed(ref, sem):
        pltpu.make_async_copy(ref, ref, sem).wait()

    def swap(p):
        return pltpu.make_async_remote_copy(
            src_ref=tiles_ref.at[0, :, quarter(dp ^ (2 + p))], dst_ref=others_ref.at[p, rows((0, 0, 0))],
            send_sem=swap_send.at[p], recv_sem=swap_recv.at[p], device_id={"dp": dp ^ (2 + p)}, device_id_type=MESH)

    def across(p, far=0):
        u = others_ref.at[p, rows((0, 0, far))]
        return pltpu.make_async_remote_copy(
            src_ref=u, dst_ref=u, send_sem=e_send.at[p], recv_sem=e_recv.at[p],
            device_id=neighbour(zyx, "x", 1), device_id_type=MESH)

    def w_copy(h, d):
        t = ((z, y)[h] + d) % 4
        dev = {"section": t} if h == 0 else {"tensor": t * 2 + x}
        return pltpu.make_async_remote_copy(
            src_ref=w_ref.at[pl.ds(pl.multiple_of(h * 4096 + t * 1024 + core * 512, 512), 512)],
            dst_ref=wz_ref.at[h, 4 - d, pl.ds(pl.multiple_of(core * 512, 512), 512)],
            send_sem=w_send.at[h, d - 1], recv_sem=w_recv.at[h, 3 - d], device_id=dev, device_id_type=MESH)

    def half(h, k, c):
        return wz_ref.at[h, k, pl.ds(pl.multiple_of(c * 512, 512), 512)]

    def c_copy(h, k):
        return pltpu.make_async_remote_copy(
            src_ref=half(h, k, core), dst_ref=half(h, k, core), send_sem=c_send.at[h, k - 1],
            recv_sem=c_recv.at[h, k - 1], device_id={"dp": dp ^ 1}, device_id_type=MESH)

    def x_copy():
        return pltpu.make_async_remote_copy(
            src_ref=all_ref.at[1], dst_ref=others_ref.at[2],
            send_sem=x_send, recv_sem=x_recv, device_id={"dp": dp ^ 1}, device_id_type=MESH)

    @pl.when(i == 0)
    def _():
        ka[...] = jnp.zeros_like(ka)
        va[...] = jnp.zeros_like(va)
        hello_all(zyx)

    for n in range(1, steps):
        def batch(n=n):
            if n == 1:
                all_said_hello()
                for p in (0, 1):
                    swap(p).start()
                for d in (1, 3):
                    for h in (0, 1):
                        w_copy(h, d).start()
                x_copy().start()
            if n == 2:
                for p in (0, 1):
                    landed(others_ref.at[p, rows((0, 0, 0))], swap_recv.at[p])
                    across(p).start()
            if n == 3:
                for p in (0, 1):
                    landed(others_ref.at[p, rows((0, 0, 1))], e_recv.at[p])
                for s in init:
                    part_copy(*s).start()
            for p, u, sends in per_step[n]:
                landed(others_ref.at[p, pair_rows(u)], recv_sem.at[p * 32 + uidx(u)])
                for s in sends:
                    part_copy(*s).start()
            if n == 9:
                for h in (0, 1):
                    w_copy(h, 2).start()
            if n == steps - 1:
                for k in (1, 3, 2):
                    for h in (0, 1):
                        landed(half(h, k, core), w_recv.at[h, k - 1])
                        c_copy(h, k).start()
        assert n >= 4 or not per_step[n]
        if n in (1, 2, 3, 9, steps - 1) or per_step[n]:
            pl.when(i == n)(batch)

    attention_rows("L", q_ref.shape[0], fac_ref[0], cnt_ref[0], q_ref, g_ref, kv_ref, dq_ref, ka, va)

    @pl.when(i == steps - 1)
    def _():
        pair_ref[:, :128] = ka[...].T.astype(BF)
        pair_ref[:, 128:] = va[...].T.astype(BF)
        for s in started:
            part_copy(*s).wait_send()
        for p in (0, 1):
            swap(p).wait_send()
        for p in (0, 1):
            across(p).wait_send()
        for h in (0, 1):
            for d in (1, 2, 3):
                w_copy(h, d).wait_send()
            for k in (1, 2, 3):
                c_copy(h, k).wait_send()
                landed(half(h, k, 1 - core), c_recv.at[h, k - 1])
        x_copy().wait()


def attention(q, g, kv, cnt, fac, tiles, every_tile, weight, R=256):
    n = q.shape[0]
    steps = n // R
    hbm = pl.BlockSpec(memory_space=pl.ANY)
    dma = pltpu.SemaphoreType.DMA
    return pl.pallas_call(
        functools.partial(attention_kernel, steps),
        grid=(steps,),
        in_specs=[pl.BlockSpec(memory_space=pltpu.SMEM)] * 2 + [
            pl.BlockSpec((R, 1024), lambda i: (i, 0)),
            pl.BlockSpec((R, 1024), lambda i: (i, 0)),
            pl.BlockSpec((512, 256), lambda i: (0, 0)), hbm, hbm, hbm],
        out_specs=[pl.BlockSpec((R, 1024), lambda i: (i, 0)), pl.BlockSpec((512, 256), lambda i: (0, 0)), hbm, hbm],
        out_shape=[jax.ShapeDtypeStruct((n, 1024), BF), jax.ShapeDtypeStruct((512, 256), BF),
                   jax.ShapeDtypeStruct((3, 512, 2048), BF), jax.ShapeDtypeStruct((2, 4, 1024, 2, 128), BF)],
        scratch_shapes=[pltpu.VMEM((128, 512), F32)] * 2 + [
            dma((count_sends(*background_plan(steps)),)), dma((64,)), dma((2,)), dma((2,)), dma((2,)), dma((2,)),
            dma((2, 3)), dma((2, 3)), dma((2, 3)), dma((2, 3)), dma, dma],
        compiler_params=pltpu.CompilerParams(
            vmem_limit_bytes=60 * 2**20, dimension_semantics=("arbitrary",), collective_id=1, has_side_effects=True),
    )(cnt, fac, q, g, kv, tiles, every_tile, weight)


def tail_kernel(pair_ref, others_ref, all_ref, wz_ref, w_ref, tg_ref, wg_ref,
                pza, pzb, pr, gq, wv, wq, tp, rs, own, xs, xr, zs,
                l_sem, p_send, p_recv, s_send, s_recv, f_send, f_recv, g_send, g_recv, h_send, h_recv,
                y_send, y_recv, x_send, x_recv, z_send, z_recv, o_sem):
    zyx = place()
    z, y, x = zyx
    dp = lax.axis_index("dp")

    def remote(src, dst, ss, rs_, dev):
        return pltpu.make_async_remote_copy(
            src_ref=src, dst_ref=dst, send_sem=ss, recv_sem=rs_, device_id=dev, device_id_type=MESH)

    hello_all(zyx)
    loads = [pltpu.make_async_copy(pair_ref, pr.at[0], l_sem.at[0]),
             pltpu.make_async_copy(all_ref.at[0], gq.at[0], l_sem.at[1]),
             pltpu.make_async_copy(others_ref.at[2], gq.at[1], l_sem.at[2]),
             pltpu.make_async_copy(others_ref.at[0], gq.at[2], l_sem.at[3]),
             pltpu.make_async_copy(others_ref.at[1], gq.at[3], l_sem.at[4])]
    for h in range(2):
        at = pl.multiple_of(h * 4096 + (z, y)[h] * 1024, 1024)
        loads.append(pltpu.make_async_copy(w_ref.at[pl.ds(at, 1024)], wv.at[h, 0], l_sem.at[5 + h * 4]))
        for k in (1, 2, 3):
            loads.append(pltpu.make_async_copy(wz_ref.at[h, k], wv.at[h, k], l_sem.at[5 + h * 4 + k]))
    for c in loads:
        c.start()
    all_said_hello()
    sends = []

    def go(c):
        c.start()
        sends.append(c)
        return c

    to2 = go(remote(pair_ref, pr.at[2], p_send.at[0], p_recv.at[0], {"dp": dp ^ 2}))
    to1 = go(remote(pair_ref, pr.at[1], p_send.at[1], p_recv.at[1], {"dp": dp ^ 1}))
    def peer(h, t):
        return {"section": t} if h == 0 else {"tensor": t * 2 + x}

    def part(ref, h, e):
        return ref.at[pl.ds(2 * e, 2)] if h == 0 else ref.at[:, pl.ds(2 * e, 2)]

    at = (z, y)
    pz = (pza, pzb)
    for e in range(2):
        for d in (1, 3, 2):
            for h in range(2):
                go(remote(part(pair_ref, h, e), pz[h].at[3 - d, e], s_send.at[h, d - 1, e], s_recv.at[h, 3 - d, e],
                          peer(h, (at[h] + d) % 4)))
    to2.wait_recv()
    to3 = go(remote(pr.at[2], pr.at[3], f_send, f_recv, {"dp": dp ^ 1}))
    to1.wait_recv()
    for c in loads[:5]:
        c.wait()
    to3.wait_recv()

    def wrows(d, j):
        return wg_ref.at[pl.ds(pl.multiple_of(d * 2048 + j * 512, 512), 512)]

    g2, g1, outs = [], [], []

    def wgrad(j):
        cols = pl.ds(j * 512, 512)
        acc = dg(pr[0].reshape(512, 256), gq[0, :, cols], 0, 0)
        for s in (1, 2, 3):
            acc = acc + dg(pr[s].reshape(512, 256), gq[s, :, cols], 0, 0)
        wq[cols] = acc.T.astype(BF).reshape(512, 2, 128)
        g2.append(go(remote(wq.at[cols], wrows(dp, j), g_send.at[0, j], g_recv.at[0, j], {"dp": dp ^ 2})))
        g1.append(go(remote(wq.at[cols], wrows(dp, j), g_send.at[1, j], g_recv.at[1, j], {"dp": dp ^ 1})))
        outs.append(pltpu.make_async_copy(wq.at[cols], wrows(dp, j), o_sem.at[2 + j]))
        outs[-1].start()

    g3 = []

    def pass_on(j):
        g2[j].wait_recv()
        g3.append(go(remote(wrows(dp ^ 2, j), wrows(dp ^ 2, j), h_send.at[j], h_recv.at[j], {"dp": dp ^ 1})))

    for c in loads[5:]:
        c.wait()
    for e in range(2):
        wgrad(e)
        for h in range(2):
            for k in range(3):
                pltpu.make_async_copy(pz[h].at[k, e], pz[h].at[k, e], s_recv.at[h, k, e]).wait()

            def tile_part(j, _, h=h, e=e):
                cols = pl.ds(pl.multiple_of(j * 512, 512), 512)
                rows = part(pr.at[0], h, e)[...].reshape(256, 256)
                acc = dg(rows, wv[h, 0, cols].reshape(512, 256), 1, 1)
                for k in range(3):
                    acc = acc + dg(pz[h][k, e].reshape(256, 256), wv[h, k + 1, cols].reshape(512, 256), 1, 1)
                t = acc.astype(BF)
                for a in range(2 if h == 0 else 4):
                    for b in range(4 if h == 0 else 2):
                        n = (a * 4 + b) if h == 0 else (a * 2 + b)
                        block = t[n * 32:(n + 1) * 32].reshape(2, 16, 512)
                        if h == 0:
                            tp[h, e, b, :, a, :, cols] = block
                        else:
                            tp[h, e, a, :, b, :, cols] = block
                return 0

            lax.fori_loop(0, 2, tile_part, 0)
            for d in (1, 3, 2):
                t = (at[1 - h] + d) % 4
                go(remote(tp.at[h, e, t], rs.at[h, e, 3 - d], y_send.at[h, e, d - 1], y_recv.at[h, e, 3 - d],
                          peer(1 - h, t)))

    wgrad(2)
    wgrad(3)
    for e in range(2):
        for h in range(2):
            for s in range(3):
                pltpu.make_async_copy(rs.at[h, e, s], rs.at[h, e, s], y_recv.at[h, e, s]).wait()
            for f in range(2):
                tot = tp[h, e, at[1 - h], f].astype(F32)
                for s in range(3):
                    tot = tot + rs[h, e, s, f].astype(F32)
                own[h, e, f] = tot
            xs[h, e] = own[h, e, 1 - x].astype(BF)
            go(remote(xs.at[h, e], xr.at[h, e], x_send.at[h, e], x_recv.at[h, e], {"tensor": y * 2 + (1 - x)}))
        pass_on(e)

    for h in range(2):
        for e in range(2):
            pltpu.make_async_copy(xr.at[h, e], xr.at[h, e], x_recv.at[h, e]).wait()
            zs[h, pl.ds(2 * e, 2)] = (own[h, e, x] + xr[h, e].astype(F32)).astype(BF)
        cols = pl.ds(pl.multiple_of(h * 4096 + at[h] * 1024, 1024), 1024)
        for d in (1, 3, 2):
            t = (at[h] + d) % 4
            go(remote(zs.at[h, t], tg_ref.at[:, cols], z_send.at[h, d - 1], z_recv.at[h, 3 - d], peer(h, t)))
        c = pltpu.make_async_copy(zs.at[h, at[h]], tg_ref.at[:, cols], o_sem.at[h])
        c.start()
        outs.append(c)

    pass_on(2)
    pass_on(3)
    for j in range(4):
        g1[j].wait_recv()
        g3[j].wait_recv()
    for h in range(2):
        for d in (1, 2, 3):
            s = (at[h] + d) % 4
            v = tg_ref.at[:, pl.ds(pl.multiple_of(h * 4096 + s * 1024, 1024), 1024)]
            pltpu.make_async_copy(v, v, z_recv.at[h, d - 1]).wait()
    for c in outs:
        c.wait()
    for c in sends:
        c.wait_send()


def tail(pair, others, every_tile, wz, weight):
    hbm = pl.BlockSpec(memory_space=pl.ANY)
    dma = pltpu.SemaphoreType.DMA
    return pl.pallas_call(
        tail_kernel,
        in_specs=[pl.BlockSpec(memory_space=pltpu.HBM)] * 5,
        out_specs=[hbm] * 2,
        out_shape=[jax.ShapeDtypeStruct((16, 8192), BF), jax.ShapeDtypeStruct((8192, 2, 128), BF)],
        scratch_shapes=[
            pltpu.VMEM((3, 2, 2, 4, 32, 256), BF), pltpu.VMEM((3, 2, 4, 2, 32, 256), BF), pltpu.VMEM((4, 4, 4, 32, 256), BF), pltpu.VMEM((4, 512, 2048), BF),
            pltpu.VMEM((2, 4, 1024, 2, 128), BF), pltpu.VMEM((2048, 2, 128), BF),
            pltpu.VMEM((2, 2, 4, 2, 2, 16, 1024), BF), pltpu.VMEM((2, 2, 3, 2, 2, 16, 1024), BF),
            pltpu.VMEM((2, 2, 2, 2, 16, 1024), F32), pltpu.VMEM((2, 2, 2, 16, 1024), BF),
            pltpu.VMEM((2, 2, 2, 16, 1024), BF), pltpu.VMEM((2, 4, 16, 1024), BF),
            dma((13,)), dma((2,)), dma((2,)), dma((2, 3, 2)), dma((2, 3, 2)), dma, dma, dma((2, 4)), dma((2, 4)), dma((4,)), dma((4,)),
            dma((2, 2, 3)), dma((2, 2, 3)), dma((2, 2)), dma((2, 2)), dma((2, 3)), dma((2, 3)), dma((6,))],
        compiler_params=pltpu.CompilerParams(
            vmem_limit_bytes=50 * 2**20, collective_id=2, has_side_effects=True),
    )(pair, others, every_tile, wz, weight)


def local(queries, grad_out, tiles, key_value_matrix, gate, tile_count):
    packed = key_value_matrix.reshape(8192, 2, 128)
    kv, quarters = gather_and_project(tiles, packed)
    query_grad, pair, others, wz = attention(
        queries[0, 0], grad_out[0, 0], kv, tile_count, jnp.tanh(gate), tiles, quarters, packed
    )
    tile_grad, weight_gradient = tail(pair.reshape(4, 4, 32, 256), others, quarters, wz, packed)
    return (query_grad[None, None], tile_grad[None], weight_gradient.reshape(1, 8192, 1, 2, 128))


def solution(mesh):
    return jax.shard_map(
        local,
        mesh=mesh,
        in_specs=(
            P("section", "dp", None, "tensor"),
            P("section", "dp", None, "tensor"),
            P("dp", ("section", "tensor"), None),
            P("section", None, "tensor", None, None),
            P("section"),
            P("dp"),
        ),
        out_specs=(
            P("section", "dp", None, "tensor"),
            P("dp", ("section", "tensor"), None),
            P("section", None, "tensor", None, None),
        ),
        check_vma=False,
    )
```
